32 devices in a mesh: row: 4 (over y, x), col: 8 (over z, core).
Axes of the slice: x: 2, y: 2, z: 4, core: 2. Of those that a mesh axis runs over, the one named last changes fastest.
Arguments:
- images: bfloat16 [704, 1152], P(('row', 'col')), may hold values from -0.1875 to 0.1875
- texts: bfloat16 [704, 1152], P(('col', 'row')), may hold values from -0.1875 to 0.1875
- logarithmic_scale: float32 [], replicated, may hold values from 2 to 3
- similarity_bias: float32 [], replicated, may hold values from -4 to -1
Outputs:
- grad_images: float32 [704, 1152], P(('row', 'col'))
- grad_texts: float32 [704, 1152], P(('col', 'row'))
The draws below stay inside these ranges and needn't reach their ends.
All inputs are finite; a program needn't handle non-finite values.
Results may differ from the reference program's by a relative error of at most 0.03.
Values may be sent and summed in bfloat16 or wider, within the bound.
A program may use at most 64 MiB of HBM per device.

```python
import jax
import jax.numpy as jnp
from jax import lax

D = 1152
BATCH = 704
ROW_BLOCK = 176
COL_BLOCK = 88
N_ROW = 4
N_COL = 8


def level_of(own_key, extent, cuts, low, top_value):
    factor_of = 1.0
    for axis_at, shards_of in cuts:
        steps = jax.random.uniform(jax.random.fold_in(jax.random.fold_in(own_key, 6), axis_at), (shards_of,), jnp.float32, low / len(cuts), top_value / len(cuts))
        factor_of = factor_of * jnp.repeat(jnp.exp(steps), extent[axis_at] // shards_of).reshape((-1,) + (1,) * (len(extent) - 1 - axis_at))
    return factor_of


def normal_values(stream_key, shape, width, limit, split=(), kind=jnp.bfloat16):
    factor_of = level_of(stream_key, shape, split, -0.22, 0.18) if split else 1.0
    array = jax.random.normal(stream_key, shape, jnp.float32) * width * factor_of
    return jnp.minimum(jnp.maximum(array, -limit), limit).astype(kind)


def setup_inputs(seed: int = 0) -> dict:
    splits = jax.random.split(jax.random.key(seed), 5)
    images = normal_values(splits[0], (BATCH, D), D ** -0.5, 0.1875, ((0, 32),))
    texts = normal_values(splits[1], (BATCH, D), D ** -0.5, 0.1875, ((0, 32),))
    logarithmic_scale = jnp.clip(jax.random.uniform(splits[2], (), jnp.float32, 2.0, 3.0), 2.0, 3.0)
    similarity_bias = jnp.clip(jax.random.uniform(splits[3], (), jnp.float32, -4.0, -1.0), -4.0, -1.0)
    return dict(images=images, texts=texts, logarithmic_scale=logarithmic_scale, similarity_bias=similarity_bias)


def normalize(values):
    wide = values.astype(jnp.float32)
    length = jnp.sqrt(lax.optimization_barrier(jnp.sum(wide * wide, axis=1, keepdims=True)) + 1e-06)
    return (wide / length, length)

def norm_back(normed, length, upstream):
    along = lax.optimization_barrier(jnp.sum(normed * upstream, axis=1, keepdims=True))
    return (upstream - normed * along) / length

def pairwise_factors(selected_entries, row_offset, column_ranges, column_offset, logit_multiplier, similarity_bias):
    similarity_logits = lax.dot_general(selected_entries, column_ranges, (((1,), (1,)), ((), ())), preferred_element_type=jnp.float32)
    row_ids = row_offset + lax.broadcasted_iota(jnp.int32, similarity_logits.shape, 0)
    col_ids = column_offset + lax.broadcasted_iota(jnp.int32, similarity_logits.shape, 1)
    pair_targets = jnp.where(row_ids == col_ids, jnp.float32(1.0), jnp.float32(-1.0))
    signed_logit = pair_targets * (logit_multiplier * similarity_logits + similarity_bias)
    return (-pair_targets * jax.nn.sigmoid(-signed_logit)).astype(jnp.bfloat16)

def reference(images, texts, logarithmic_scale, similarity_bias):
    img_unit, img_len = normalize(images)
    txt_unit, txt_len = normalize(texts)
    img_bf = img_unit.astype(jnp.bfloat16)
    caption_halfprecision = txt_unit.astype(jnp.bfloat16)
    logit_multiplier = jnp.exp(logarithmic_scale)

    def one_block(carry, block_index):
        begin_offset = (block_index * ROW_BLOCK).astype(jnp.int32)
        selected_entries = lax.dynamic_slice_in_dim(img_bf, begin_offset, ROW_BLOCK, 0)
        sigmoid_factors = pairwise_factors(selected_entries, begin_offset, caption_halfprecision, jnp.int32(0), logit_multiplier, similarity_bias)
        partial_results = jnp.einsum('rgc,gcd->grd', sigmoid_factors.reshape(ROW_BLOCK, N_COL, COL_BLOCK).astype(jnp.float32), caption_halfprecision.reshape(N_COL, COL_BLOCK, D).astype(jnp.float32))
        img_rows = lax.optimization_barrier(jnp.sum(logit_multiplier * partial_results, axis=0))
        caption_portion = logit_multiplier * lax.dot_general(sigmoid_factors, selected_entries, (((0,), (0,)), ((), ())), preferred_element_type=jnp.float32)
        caption_portion = lax.optimization_barrier(caption_portion.astype(jnp.bfloat16))
        return (carry + caption_portion.astype(jnp.float32), img_rows)
    start_carry = jnp.zeros((BATCH, D), jnp.float32)
    grad_txt_unit, img_blocks = lax.scan(one_block, start_carry, jnp.arange(N_ROW, dtype=jnp.int32))
    grad_img_unit = img_blocks.reshape(BATCH, D)
    return (norm_back(img_unit, img_len, grad_img_unit), norm_back(txt_unit, txt_len, grad_txt_unit))
```

```python
import functools

import jax
import jax.numpy as jnp
from jax import lax
from jax.experimental import pallas as pl
from jax.experimental.pallas import tpu as pltpu
from jax.sharding import PartitionSpec as P

MESH = pl.DeviceIdType.MESH
F32, BF16 = jnp.float32, jnp.bfloat16


def unit_rows(x_ref, wide, length_ref, unit_ref):
    rows = x_ref.shape[0]
    wide[...] = jnp.zeros_like(wide)
    wide[:rows] = x_ref[...].astype(F32)
    x = wide[...]
    length = jnp.sqrt(jnp.sum(x * x, axis=1, keepdims=True) + 1e-06)
    unit = x / length
    unit_ref[...] = unit
    length_ref[...] = jnp.broadcast_to(length, length_ref.shape)
    return unit.astype(BF16)


def norm_back(unit, length, upstream):
    along = jnp.sum(unit * upstream, axis=1, keepdims=True)
    return (upstream - unit * along) / length


def kernel(n_row, n_col, cores, img_ref, txt_ref, scale_ref, bias_ref, gimg_ref, gtxt_ref,
           wide, iu, tu, il, tl, gi, gt, wt, pi, pt, ri, rt,
           si, ci, st, ct, si2, ci2, st2, ct2):
    rows = img_ref.shape[0]
    pad = gi.shape[1]
    n_i, n_t = n_row * cores, n_col // cores
    row, col = lax.axis_index("row"), lax.axis_index("col")
    plane, core = col // cores, col % cores
    me_i, me_t = row * cores + core, plane

    def at_i(g):
        return (g // cores, plane * cores + g % cores)

    def at_t(h):
        return (row, h * cores + core)

    to_i = [lax.rem(me_i + k, n_i) for k in range(1, n_i)]
    to_t = [lax.rem(me_t + k, n_t) for k in range(1, n_t)]

    barrier = pltpu.get_barrier_semaphore()
    for h in to_t:
        pl.semaphore_signal(barrier, inc=1, device_id=at_t(h), device_id_type=MESH)
    for g in to_i:
        pl.semaphore_signal(barrier, inc=1, device_id=at_i(g), device_id_type=MESH)
    gt[me_t] = unit_rows(txt_ref, wide, tl, tu)
    gi[me_i] = unit_rows(img_ref, wide, il, iu)
    pl.semaphore_wait(barrier, n_i + n_t - 2)

    def spread(src_of, dst, mine, partners, place, send, recv):
        copies = []
        for k, other in enumerate(partners):
            copy = pltpu.make_async_remote_copy(
                src_ref=src_of(other), dst_ref=dst.at[mine],
                send_sem=send.at[k], recv_sem=recv.at[mine],
                device_id=place(other), device_id_type=MESH)
            copy.start()
            copies.append(copy)
        return copies

    def arrived(dst, other, recv, send):
        pltpu.make_async_remote_copy(
            src_ref=dst.at[other], dst_ref=dst.at[other],
            send_sem=send.at[0], recv_sem=recv.at[other],
            device_id=(row, col), device_id_type=MESH).wait_recv()

    sent = spread(lambda h: gt.at[me_t], gt, me_t, to_t, at_t, st, ct)
    sent += spread(lambda g: gi.at[me_i], gi, me_i, to_i, at_i, si, ci)
    for h in to_t:
        arrived(gt, h, ct, st)
    for g in to_i:
        arrived(gi, g, ci, si)

    images = gi[...].reshape(n_i * pad, -1)
    texts = gt[...].reshape(n_t * pad, -1)
    temperature = jnp.exp(jnp.full((1, 1), scale_ref[0], F32))
    scores = lax.dot_general(images, texts, (((1,), (1,)), ((), ())), preferred_element_type=F32)
    r = lax.broadcasted_iota(jnp.int32, scores.shape, 0)
    c = lax.broadcasted_iota(jnp.int32, scores.shape, 1)
    g, h = r // pad, c // pad
    row_ids = ((g // cores) * n_col + plane * cores + g % cores) * rows + r % pad
    col_ids = ((h * cores + core) * n_row + row) * rows + c % pad
    label = jnp.where(row_ids == col_ids, F32(1.0), F32(-1.0))
    margin = label * (temperature * scores + bias_ref[0])
    weights = -label * jax.nn.sigmoid(-margin)
    wt[...] = weights.T.astype(BF16)
    pt[...] = jnp.dot(wt[...], images, preferred_element_type=F32).astype(BF16).reshape(pt.shape)
    sent += spread(lambda h: pt.at[h], rt, me_t, to_t, at_t, st2, ct2)
    pi[...] = jnp.dot(weights.astype(BF16), texts, preferred_element_type=F32).astype(BF16).reshape(pi.shape)
    sent += spread(lambda g: pi.at[g], ri, me_i, to_i, at_i, si2, ci2)

    total = pt[me_t].astype(F32)
    for h in to_t:
        arrived(rt, h, ct2, st2)
        total += rt[h].astype(F32)
    gtxt_ref[...] = norm_back(tu[...], tl[:, :1], temperature * total)[:rows]
    total = pi[me_i].astype(F32)
    for g in to_i:
        arrived(ri, g, ci2, si2)
        total += ri[g].astype(F32)
    gimg_ref[...] = norm_back(iu[...], il[:, :1], temperature * total)[:rows]
    for copy in sent:
        copy.wait_send()


def on_device(n_row, n_col, images, texts, logarithmic_scale, similarity_bias):
    rows, width = images.shape
    pad = -(-rows // 16) * 16
    cores = 2 if n_col % 2 == 0 else 1
    n_i, n_t = n_row * cores, n_col // cores
    vmem = pl.BlockSpec(memory_space=pltpu.VMEM)
    smem = pl.BlockSpec(memory_space=pltpu.SMEM)
    out = jax.ShapeDtypeStruct((rows, width), F32)
    dma = pltpu.SemaphoreType.DMA
    return pl.pallas_call(
        functools.partial(kernel, n_row, n_col, cores),
        out_shape=(out, out),
        in_specs=[vmem, vmem, smem, smem],
        out_specs=(vmem, vmem),
        scratch_shapes=[
            pltpu.VMEM((pad, width), F32),
            pltpu.VMEM((pad, width), F32),
            pltpu.VMEM((pad, width), F32),
            pltpu.VMEM((pad, 128), F32),
            pltpu.VMEM((pad, 128), F32),
            pltpu.VMEM((n_i, pad, width), BF16),
            pltpu.VMEM((n_t, pad, width), BF16),
            pltpu.VMEM((n_t * pad, n_i * pad), BF16),
            pltpu.VMEM((n_i, pad, width), BF16),
            pltpu.VMEM((n_t, pad, width), BF16),
            pltpu.VMEM((n_i, pad, width), BF16),
            pltpu.VMEM((n_t, pad, width), BF16),
            dma((n_i,)), dma((n_i,)), dma((n_t,)), dma((n_t,)),
            dma((n_i,)), dma((n_i,)), dma((n_t,)), dma((n_t,)),
        ],
        compiler_params=pltpu.CompilerParams(
            collective_id=0, has_side_effects=True, vmem_limit_bytes=48 * 2**20),
    )(images, texts, logarithmic_scale.reshape(1), similarity_bias.reshape(1))


def solution(mesh):
    return jax.shard_map(
        functools.partial(on_device, mesh.shape["row"], mesh.shape["col"]),
        mesh=mesh,
        in_specs=(P(("row", "col"), None), P(("col", "row"), None), P(), P()),
        out_specs=(P(("row", "col"), None), P(("col", "row"), None)),
        check_vma=False,
    )
```

```python
import functools

import jax
import jax.numpy as jnp
from jax import lax
from jax.experimental import pallas as pl
from jax.experimental.pallas import tpu as pltpu
from jax.sharding import PartitionSpec as P

MESH = pl.DeviceIdType.MESH
F32, BF16 = jnp.float32, jnp.bfloat16


def pack(x):
    width = x.shape[1]
    left = -(-width // 256) * 128
    right = jnp.concatenate([x[16:, left:], jnp.zeros((8, 2 * left - width), x.dtype)], axis=1)
    return x[:16], jnp.concatenate([x[16:, :left], right], axis=0)


def unpack_tail(tail, width):
    left = tail.shape[1]
    return jnp.concatenate([tail[:8], tail[8:, :width - left]], axis=1)


def unit_rows(x_ref, wide, length_ref, unit_ref, block_ref):
    rows, width = x_ref.shape
    wide[...] = jnp.zeros_like(wide)
    wide[:rows] = x_ref[...].astype(F32)
    x = wide[...]
    length = jnp.sqrt(jnp.sum(x * x, axis=1, keepdims=True) + 1e-06)
    unit = x / length
    unit_ref[...] = unit
    length_ref[...] = jnp.broadcast_to(length, length_ref.shape)
    head, tail = pack(unit)
    block_ref[:, :width] = head.astype(BF16)
    block_ref[:, width:] = tail.astype(BF16)


def all_rows(blocks, width):
    n = blocks.shape[0]
    heads = blocks[:, :, :width].reshape(n * 16, width)
    tails = [unpack_tail(blocks[k, :, width:].astype(F32), width) for k in range(n)]
    return jnp.concatenate([heads, jnp.concatenate(tails, axis=0).astype(BF16)], axis=0)


def to_blocks(partial, blocks):
    n, width = blocks.shape[0], partial.shape[1]
    for k in range(n):
        head, tail = pack(jnp.concatenate(
            [partial[16 * k:16 * k + 16], partial[16 * n + 8 * k:16 * n + 8 * k + 8]], axis=0))
        blocks[k, :, :width] = head.astype(BF16)
        blocks[k, :, width:] = tail.astype(BF16)


def member_row(index, n):
    tail = index - 16 * n
    member = jnp.where(index < 16 * n, index // 16, tail // 8)
    return member, jnp.where(index < 16 * n, index % 16, 16 + tail % 8)


def norm_back(unit, length, upstream):
    along = jnp.sum(unit * upstream, axis=1, keepdims=True)
    return (upstream - unit * along) / length


def kernel(n_row, n_col, cores, img_ref, txt_ref, scale_ref, bias_ref, gimg_ref, gtxt_ref,
           xi, xt, wide, iu, tu, il, tl, gi, gt, wt, pi, pt, ri, rt,
           in_sem, si, ci, st, ct, si2, ci2, st2, ct2):
    rows, width = img_ref.shape
    load_t = pltpu.make_async_copy(txt_ref, xt, in_sem.at[0])
    load_i = pltpu.make_async_copy(img_ref, xi, in_sem.at[1])
    load_t.start()
    load_i.start()
    n_i, n_t = n_row * cores, n_col // cores
    row, col = lax.axis_index("row"), lax.axis_index("col")
    plane, core = col // cores, col % cores
    me_i, me_t = row * cores + core, plane

    def at_i(g):
        return (g // cores, plane * cores + g % cores)

    def at_t(h):
        return (row, h * cores + core)

    to_i = [lax.rem(me_i + k, n_i) for k in range(1, n_i)]
    to_t = [lax.rem(me_t + k, n_t) for k in range(1, n_t)]

    barrier = pltpu.get_barrier_semaphore()
    for h in to_t:
        pl.semaphore_signal(barrier, inc=1, device_id=at_t(h), device_id_type=MESH)
    for g in to_i:
        pl.semaphore_signal(barrier, inc=1, device_id=at_i(g), device_id_type=MESH)
    load_t.wait()
    unit_rows(xt, wide, tl, tu, gt.at[me_t])
    load_i.wait()
    unit_rows(xi, wide, il, iu, gi.at[me_i])
    pl.semaphore_wait(barrier, n_i + n_t - 2)

    def spread(src_of, dst, mine, partners, place, send, recv):
        copies = []
        for k, other in enumerate(partners):
            copy = pltpu.make_async_remote_copy(
                src_ref=src_of(other), dst_ref=dst.at[mine],
                send_sem=send.at[k], recv_sem=recv.at[mine],
                device_id=place(other), device_id_type=MESH)
            copy.start()
            copies.append(copy)
        return copies

    def arrived(dst, other, recv, send):
        pltpu.make_async_remote_copy(
            src_ref=dst.at[other], dst_ref=dst.at[other],
            send_sem=send.at[0], recv_sem=recv.at[other],
            device_id=(row, col), device_id_type=MESH).wait_recv()

    sent = spread(lambda h: gt.at[me_t], gt, me_t, to_t, at_t, st, ct)
    sent += spread(lambda g: gi.at[me_i], gi, me_i, to_i, at_i, si, ci)
    for h in to_t:
        arrived(gt, h, ct, st)
    for g in to_i:
        arrived(gi, g, ci, si)

    images = all_rows(gi, width)
    texts = all_rows(gt, width)
    temperature = jnp.exp(jnp.full((1, 1), scale_ref[0], F32))
    scores = lax.dot_general(images, texts, (((1,), (1,)), ((), ())), preferred_element_type=F32)
    r = lax.broadcasted_iota(jnp.int32, scores.shape, 0)
    c = lax.broadcasted_iota(jnp.int32, scores.shape, 1)
    g, r = member_row(r, n_i)
    h, c = member_row(c, n_t)
    row_ids = ((g // cores) * n_col + plane * cores + g % cores) * rows + r
    col_ids = ((h * cores + core) * n_row + row) * rows + c
    label = jnp.where(row_ids == col_ids, F32(1.0), F32(-1.0))
    margin = label * (temperature * scores + bias_ref[0])
    weights = -label * jax.nn.sigmoid(-margin)
    wt[...] = weights.T.astype(BF16)
    to_blocks(jnp.dot(wt[...], images, preferred_element_type=F32), pt)
    sent += spread(lambda h: pt.at[h], rt, me_t, to_t, at_t, st2, ct2)
    to_blocks(jnp.dot(weights.astype(BF16), texts, preferred_element_type=F32), pi)
    sent += spread(lambda g: pi.at[g], ri, me_i, to_i, at_i, si2, ci2)

    def rows_of(total):
        return temperature * jnp.concatenate([total[:, :width], unpack_tail(total[:, width:], width)], axis=0)

    total = pt[me_t].astype(F32)
    for h in to_t:
        arrived(rt, h, ct2, st2)
        total += rt[h].astype(F32)
    gtxt_ref[...] = norm_back(tu[...], tl[:, :1], rows_of(total))[:rows]
    total = pi[me_i].astype(F32)
    for g in to_i:
        arrived(ri, g, ci2, si2)
        total += ri[g].astype(F32)
    gimg_ref[...] = norm_back(iu[...], il[:, :1], rows_of(total))[:rows]
    for copy in sent:
        copy.wait_send()


def on_device(n_row, n_col, images, texts, logarithmic_scale, similarity_bias):
    rows, width = images.shape
    pad = 24
    packed = width + -(-width // 256) * 128
    assert 16 < rows <= pad
    cores = 2 if n_col % 2 == 0 else 1
    n_i, n_t = n_row * cores, n_col // cores
    vmem = pl.BlockSpec(memory_space=pltpu.VMEM)
    hbm = pl.BlockSpec(memory_space=pltpu.HBM)
    smem = pl.BlockSpec(memory_space=pltpu.SMEM)
    out = jax.ShapeDtypeStruct((rows, width), F32)
    dma = pltpu.SemaphoreType.DMA
    return pl.pallas_call(
        functools.partial(kernel, n_row, n_col, cores),
        out_shape=(out, out),
        in_specs=[hbm, hbm, smem, smem],
        out_specs=(vmem, vmem),
        scratch_shapes=[
            pltpu.VMEM((rows, width), BF16),
            pltpu.VMEM((rows, width), BF16),
            pltpu.VMEM((pad, width), F32),
            pltpu.VMEM((pad, width), F32),
            pltpu.VMEM((pad, width), F32),
            pltpu.VMEM((pad, 128), F32),
            pltpu.VMEM((pad, 128), F32),
            pltpu.VMEM((n_i, 16, packed), BF16),
            pltpu.VMEM((n_t, 16, packed), BF16),
            pltpu.VMEM((n_t * pad, n_i * pad), BF16),
            pltpu.VMEM((n_i, 16, packed), BF16),
            pltpu.VMEM((n_t, 16, packed), BF16),
            pltpu.VMEM((n_i, 16, packed), BF16),
            pltpu.VMEM((n_t, 16, packed), BF16),
            dma((2,)),
            dma((n_i,)), dma((n_i,)), dma((n_t,)), dma((n_t,)),
            dma((n_i,)), dma((n_i,)), dma((n_t,)), dma((n_t,)),
        ],
        compiler_params=pltpu.CompilerParams(
            collective_id=0, has_side_effects=True),
    )(images, texts, logarithmic_scale.reshape(1), similarity_bias.reshape(1))


def solution(mesh):
    return jax.shard_map(
        functools.partial(on_device, mesh.shape["row"], mesh.shape["col"]),
        mesh=mesh,
        in_specs=(P(("row", "col"), None), P(("col", "row"), None), P(), P()),
        out_specs=(P(("row", "col"), None), P(("col", "row"), None)),
        check_vma=False,
    )
```

```python
import functools

import jax
import jax.numpy as jnp
from jax import lax
from jax.experimental import pallas as pl
from jax.experimental.pallas import tpu as pltpu
from jax.sharding import PartitionSpec as P

MESH = pl.DeviceIdType.MESH
F32, BF16 = jnp.float32, jnp.bfloat16


def pack(x):
    width = x.shape[1]
    left = -(-width // 256) * 128
    right = jnp.concatenate([x[16:, left:], jnp.zeros((8, 2 * left - width), x.dtype)], axis=1)
    return x[:16], jnp.concatenate([x[16:, :left], right], axis=0)


def unpack_tail(tail, width):
    left = tail.shape[1]
    return jnp.concatenate([tail[:8], tail[8:, :width - left]], axis=1)


def unit_rows(x_ref, wide, length_ref, unit_ref, block_ref):
    rows, width = x_ref.shape
    wide[...] = jnp.zeros_like(wide)
    wide[:rows] = x_ref[...].astype(F32)
    x = wide[...]
    length = jnp.sqrt(jnp.sum(x * x, axis=1, keepdims=True) + 1e-06)
    unit = x / length
    unit_ref[...] = unit
    length_ref[...] = jnp.broadcast_to(length, length_ref.shape)
    head, tail = pack(unit)
    block_ref[:, :width] = head.astype(BF16)
    block_ref[:, width:] = tail.astype(BF16)


def all_rows(blocks, width):
    n = blocks.shape[0]
    heads = blocks[:, :, :width].reshape(n * 16, width)
    tails = [unpack_tail(blocks[k, :, width:].astype(F32), width) for k in range(n)]
    return jnp.concatenate([heads, jnp.concatenate(tails, axis=0).astype(BF16)], axis=0)


def to_blocks(partial, blocks):
    n, width = blocks.shape[0], partial.shape[1]
    for k in range(n):
        head, tail = pack(jnp.concatenate(
            [partial[16 * k:16 * k + 16], partial[16 * n + 8 * k:16 * n + 8 * k + 8]], axis=0))
        blocks[k, :, :width] = head.astype(blocks.dtype)
        blocks[k, :, width:] = tail.astype(blocks.dtype)


def member_row(index, n):
    tail = index - 16 * n
    member = jnp.where(index < 16 * n, index // 16, tail // 8)
    return member, jnp.where(index < 16 * n, index % 16, 16 + tail % 8)


def norm_back(unit, length, upstream):
    along = jnp.sum(unit * upstream, axis=1, keepdims=True)
    return (upstream - unit * along) / length


def kernel(n_row, n_t, img_ref, txt_ref, scale_ref, bias_ref, gimg_ref, gtxt_ref,
           xi, xt, wide, iu, tu, il, tl, gi, gt, wt, wh, wl, pt, ps, po, pi, acc, rt, rl, rs, ri,
           in_sem, send_sem, ci, ct, ct2, ci2, pair_sem):
    rows, width = img_ref.shape
    load_t = pltpu.make_async_copy(txt_ref, xt, in_sem.at[0])
    load_i = pltpu.make_async_copy(img_ref, xi, in_sem.at[1])
    load_t.start()
    load_i.start()
    n_i = 2 * n_row
    row, col = lax.axis_index("row"), lax.axis_index("col")
    plane, core = col // 2, col % 2
    other_core = 1 - core
    me_i = core * n_row + row
    line = n_t == 4
    first_end, last_end = plane == 0, plane == n_t - 1
    relay = jnp.logical_or(plane == 1, plane == 2)
    far_end = jnp.where(plane == 1, 3, 0)
    near_end = jnp.where(plane == 1, 0, 3)

    def at_row(r):
        return (r, col)

    def at_plane(h):
        return (row, 2 * h + core)

    sibling = (row, 2 * plane + other_core)
    other_rows = [lax.rem(row + k, n_row) for k in range(1, n_row)]
    planes = {k: lax.rem(plane + k, n_t) for k in range(1, n_t)}
    order = [2, 3, 1] if line else list(planes)

    barrier = pltpu.get_barrier_semaphore()
    for place in [at_plane(planes[k]) for k in order] + [at_row(r) for r in other_rows] + [sibling]:
        pl.semaphore_signal(barrier, inc=1, device_id=place, device_id_type=MESH)
    load_t.wait()
    unit_rows(xt, wide, tl, tu, gt.at[plane])
    load_i.wait()
    unit_rows(xi, wide, il, iu, gi.at[me_i])
    pl.semaphore_wait(barrier, n_row + n_t - 1)

    sent = []

    def when(condition):
        return pl.when(condition) if condition is not None else lambda f: f()

    def push(src, dst, recv, place, condition=None):
        slot = send_sem.at[len(sent)]

        def copy():
            return pltpu.make_async_remote_copy(
                src_ref=src, dst_ref=dst, send_sem=slot, recv_sem=recv,
                device_id=place, device_id_type=MESH)

        when(condition)(lambda: copy().start())
        sent.append((copy, condition))

    def arrived(dst, recv, condition=None):
        when(condition)(lambda: pltpu.make_async_remote_copy(
            src_ref=dst, dst_ref=dst, send_sem=send_sem.at[0], recv_sem=recv,
            device_id=sibling, device_id_type=MESH).wait_recv())

    def direct(k):
        if not line or k == 2:
            return None
        return jnp.logical_not(last_end if k == 1 else first_end)

    for k in order:
        push(gt.at[plane], gt.at[plane], ct.at[plane], at_plane(planes[k]), direct(k))
    for r in other_rows:
        push(gi.at[me_i], gi.at[me_i], ci.at[me_i], at_row(r))
    push(gi.at[me_i], gi.at[me_i], ci.at[me_i], sibling)
    for k, r in enumerate(other_rows):
        g = core * n_row + r
        arrived(gi.at[g], ci.at[g])
        push(gi.at[g], gi.at[g], ci.at[g], sibling)
        if line and k == 0:
            h = planes[2]
            arrived(gt.at[h], ct.at[h])
            push(gt.at[far_end], gt.at[far_end], ct.at[far_end], at_plane(near_end), relay)
    for k in order:
        if not (line and k == 2):
            arrived(gt.at[planes[k]], ct.at[planes[k]])
    for r in [row] + other_rows:
        g = other_core * n_row + r
        arrived(gi.at[g], ci.at[g])

    images = all_rows(gi, width)
    texts = all_rows(gt, width)
    temperature = jnp.exp(jnp.full((1, 1), scale_ref[0], F32))
    scores = lax.dot_general(images, texts, (((1,), (1,)), ((), ())), preferred_element_type=F32)
    r = lax.broadcasted_iota(jnp.int32, scores.shape, 0)
    c = lax.broadcasted_iota(jnp.int32, scores.shape, 1)
    g, r = member_row(r, n_i)
    h, c = member_row(c, n_t)
    row_ids = ((g % n_row) * (2 * n_t) + plane * 2 + g // n_row) * rows + r
    col_ids = ((h * 2 + core) * n_row + row) * rows + c
    label = jnp.where(row_ids == col_ids, F32(1.0), F32(-1.0))
    margin = label * (temperature * scores + bias_ref[0])
    weights = -label * jax.nn.sigmoid(-margin)
    wt[...] = weights.T.astype(BF16)
    wh[...] = weights[:16 * n_i].astype(BF16)
    wl[...] = weights[16 * n_i:].astype(BF16)

    to_blocks(jnp.dot(wt[...], images, preferred_element_type=F32), pt)
    if line:
        end = jnp.logical_or(first_end, last_end)
        opposite = jnp.where(first_end, 3, 0)
        push(pt.at[opposite], rl, pair_sem.at[1], at_plane(jnp.where(first_end, 1, 2)), end)
        through = jnp.logical_not(relay)
    for k in order:
        push(pt.at[planes[k]], rt.at[plane], ct2.at[plane], at_plane(planes[k]),
             through if line and k == 2 else direct(k))

    def half(c):
        head = wh[pl.ds(pl.multiple_of(c * (16 * n_row), 16), 16 * n_row)]
        tail = wl[pl.ds(pl.multiple_of(c * (8 * n_row), 16), 8 * n_row)]
        return jnp.dot(jnp.concatenate([head, tail], axis=0), texts, preferred_element_type=F32)

    to_blocks(half(other_core), ps)
    push(ps, rs, pair_sem.at[0], sibling)
    to_blocks(half(core), po)
    arrived(rs, pair_sem.at[0])
    for r in other_rows:
        pi[r] = (po[r] + rs[r].astype(F32)).astype(BF16)
        push(pi.at[r], ri.at[row], ci2.at[row], at_row(r))
    if line:
        @pl.when(relay)
        def _():
            arrived(rl, pair_sem.at[1])
            pt[far_end] = (pt[far_end].astype(F32) + rl[...].astype(F32)).astype(BF16)
        push(pt.at[far_end], rt.at[plane], ct2.at[plane], at_plane(far_end), relay)

    def rows_of(total):
        return temperature * jnp.concatenate([total[:, :width], unpack_tail(total[:, width:], width)], axis=0)

    acc[...] = po[row] + rs[row].astype(F32)
    for r in other_rows:
        arrived(ri.at[r], ci2.at[r])
        acc[...] += ri[r].astype(F32)
    gimg_ref[...] = norm_back(iu[...], il[:, :1], rows_of(acc[...]))[:rows]
    acc[...] = pt[plane].astype(F32)
    for k in order[1:] + order[:1]:
        h = planes[k]

        def add(h=h):
            arrived(rt.at[h], ct2.at[h])
            acc[...] += rt[h].astype(F32)

        when(direct(k))(add)
    gtxt_ref[...] = norm_back(tu[...], tl[:, :1], rows_of(acc[...]))[:rows]
    for copy, condition in sent:
        when(condition)(lambda copy=copy: copy().wait_send())


def on_device(n_row, n_col, images, texts, logarithmic_scale, similarity_bias):
    rows, width = images.shape
    pad = 24
    packed = width + -(-width // 256) * 128
    assert 16 < rows <= pad and n_col % 2 == 0 and n_row % 2 == 0
    n_i, n_t = 2 * n_row, n_col // 2
    vmem = pl.BlockSpec(memory_space=pltpu.VMEM)
    hbm = pl.BlockSpec(memory_space=pltpu.HBM)
    smem = pl.BlockSpec(memory_space=pltpu.SMEM)
    out = jax.ShapeDtypeStruct((rows, width), F32)
    dma = pltpu.SemaphoreType.DMA

    def blocks(n, kind=BF16):
        return pltpu.VMEM((n, 16, packed), kind)

    return pl.pallas_call(
        functools.partial(kernel, n_row, n_t),
        out_shape=(out, out),
        in_specs=[hbm, hbm, smem, smem],
        out_specs=(vmem, vmem),
        scratch_shapes=[
            pltpu.VMEM((rows, width), BF16),
            pltpu.VMEM((rows, width), BF16),
            pltpu.VMEM((pad, width), F32),
            pltpu.VMEM((pad, width), F32),
            pltpu.VMEM((pad, width), F32),
            pltpu.VMEM((pad, 128), F32),
            pltpu.VMEM((pad, 128), F32),
            blocks(n_i),
            blocks(n_t),
            pltpu.VMEM((n_t * pad, n_i * pad), BF16),
            pltpu.VMEM((n_i * 16, n_t * pad), BF16),
            pltpu.VMEM((n_i * 8, n_t * pad), BF16),
            blocks(n_t),
            blocks(n_row),
            blocks(n_row, F32),
            blocks(n_row),
            pltpu.VMEM((16, packed), F32),
            blocks(n_t),
            pltpu.VMEM((16, packed), BF16),
            blocks(n_row),
            blocks(n_row),
            dma((2,)), dma((3 * n_row + 2 * n_t + 2,)),
            dma((n_i,)), dma((n_t,)), dma((n_t,)), dma((n_row,)), dma((2,)),
        ],
        compiler_params=pltpu.CompilerParams(
            collective_id=0, has_side_effects=True),
    )(images, texts, logarithmic_scale.reshape(1), similarity_bias.reshape(1))


def solution(mesh):
    return jax.shard_map(
        functools.partial(on_device, mesh.shape["row"], mesh.shape["col"]),
        mesh=mesh,
        in_specs=(P(("row", "col"), None), P(("col", "row"), None), P(), P()),
        out_specs=(P(("row", "col"), None), P(("col", "row"), None)),
        check_vma=False,
    )
```

```python
import functools

import jax
import jax.numpy as jnp
from jax import lax
from jax.experimental import pallas as pl
from jax.experimental.pallas import tpu as pltpu
from jax.sharding import PartitionSpec as P

MESH = pl.DeviceIdType.MESH
F32, BF16 = jnp.float32, jnp.bfloat16


def pack(x):
    width = x.shape[1]
    left = -(-width // 256) * 128
    right = jnp.concatenate([x[16:, left:], jnp.zeros((8, 2 * left - width), x.dtype)], axis=1)
    return x[:16], jnp.concatenate([x[16:, :left], right], axis=0)


def unpack_tail(tail, width):
    left = tail.shape[1]
    return jnp.concatenate([tail[:8], tail[8:, :width - left]], axis=1)


def unit_rows(x):
    length = jnp.sqrt(jnp.sum(x * x, axis=1, keepdims=True) + 1e-06)
    return x * (1.0 / length), length


def to_blocks(partial, blocks):
    width = partial.shape[1]
    for k in range(blocks.shape[0]):
        head, tail = pack(partial[24 * k:24 * k + 24])
        blocks[k, :, :width] = head.astype(blocks.dtype)
        blocks[k, :, width:] = tail.astype(blocks.dtype)


def member_row(index):
    member = lax.shift_right_logical(index * 43691, jnp.full_like(index, 20))
    return member, index - 24 * member


def norm_back(unit, length, upstream):
    along = jnp.sum(unit * upstream, axis=1, keepdims=True)
    return (upstream - unit * along) / length


def kernel(n_row, n_t, img_ref, txt_ref, scale_ref, bias_ref, gimg_ref, gtxt_ref,
           oi, ot, iu, tu, il, tl, gi, gt, wt, w, pt, ps, po, pi, acc, rt, rl, rs, ri,
           in_sem, out_sem, send_sem, ci, ct, ct2, ci2, pair_sem):
    rows, width = img_ref.shape
    n_i = 2 * n_row
    row, col = lax.axis_index("row"), lax.axis_index("col")
    plane, core = col // 2, col % 2
    other_core = 1 - core
    me_i = core * n_row + row
    line = n_t == 4
    first_end, last_end = plane == 0, plane == n_t - 1
    relay = jnp.logical_or(plane == 1, plane == 2)
    far_end = jnp.where(plane == 1, 3, 0)
    near_end = jnp.where(plane == 1, 0, 3)

    def at_row(r):
        return (r, col)

    def at_plane(h):
        return (row, 2 * h + core)

    sibling = (row, 2 * plane + other_core)
    other_rows = [lax.rem(row + k, n_row) for k in range(1, n_row)]
    planes = {k: lax.rem(plane + k, n_t) for k in range(1, n_t)}
    order = [2, 3, 1] if line else list(planes)

    barrier = pltpu.get_barrier_semaphore()
    for place in [at_plane(planes[k]) for k in order] + [at_row(r) for r in other_rows] + [sibling]:
        pl.semaphore_signal(barrier, inc=1, device_id=place, device_id_type=MESH)
    load_t = pltpu.make_async_copy(txt_ref, gt.at[plane], in_sem.at[0])
    load_i = pltpu.make_async_copy(img_ref, gi.at[me_i], in_sem.at[1])
    load_t.start()
    load_i.start()
    iu[...] = jnp.zeros_like(iu)
    tu[...] = jnp.zeros_like(tu)
    pl.semaphore_wait(barrier, n_row + n_t - 1)

    sent = []

    def when(condition):
        return pl.when(condition) if condition is not None else lambda f: f()

    def push(src, dst, recv, place, condition=None):
        slot = send_sem.at[len(sent)]

        def copy():
            return pltpu.make_async_remote_copy(
                src_ref=src, dst_ref=dst, send_sem=slot, recv_sem=recv,
                device_id=place, device_id_type=MESH)

        when(condition)(lambda: copy().start())
        sent.append((copy, condition))

    def arrived(dst, recv, condition=None):
        when(condition)(lambda: pltpu.make_async_remote_copy(
            src_ref=dst, dst_ref=dst, send_sem=send_sem.at[0], recv_sem=recv,
            device_id=sibling, device_id_type=MESH).wait_recv())

    def direct(k):
        if not line or k == 2:
            return None
        return jnp.logical_not(last_end if k == 1 else first_end)

    for k in order:
        push(txt_ref, gt.at[plane], ct.at[plane], at_plane(planes[k]), direct(k))
    for r in other_rows:
        push(img_ref, gi.at[me_i], ci.at[me_i], at_row(r))
    push(img_ref, gi.at[me_i], ci.at[me_i], sibling)

    def normalise(blocks, g, units, length_ref=None):
        at = pl.multiple_of(g * 24, 8)
        units[pl.ds(at, rows)] = blocks[g].astype(F32)
        unit, length = unit_rows(units[pl.ds(at, 24)])
        units[pl.ds(at, 24)] = unit
        if length_ref is not None:
            length_ref[...] = jnp.broadcast_to(length, length_ref.shape)

    load_t.wait()
    normalise(gt, plane, tu, tl)
    load_i.wait()
    normalise(gi, me_i, iu, il)
    for k, r in enumerate(other_rows):
        g = core * n_row + r
        arrived(gi.at[g], ci.at[g])
        push(gi.at[g], gi.at[g], ci.at[g], sibling)
        if line and k == 0:
            h = planes[2]
            arrived(gt.at[h], ct.at[h])
            push(gt.at[far_end], gt.at[far_end], ct.at[far_end], at_plane(near_end), relay)
    for r in other_rows:
        normalise(gi, core * n_row + r, iu)
    for r in [row] + other_rows:
        g = other_core * n_row + r
        arrived(gi.at[g], ci.at[g])
        normalise(gi, g, iu)
    images = iu[...].astype(BF16)
    for k in order:
        if not (line and k == 2):
            arrived(gt.at[planes[k]], ct.at[planes[k]])
        normalise(gt, planes[k], tu)
    texts = tu[...].astype(BF16)
    temperature = jnp.exp(jnp.full((1, 1), scale_ref[...], F32))
    scores = lax.dot_general(images, texts, (((1,), (1,)), ((), ())), preferred_element_type=F32)
    r = lax.broadcasted_iota(jnp.int32, (scores.shape[0], 1), 0)
    c = lax.broadcasted_iota(jnp.int32, (1, scores.shape[1]), 1)
    g, r = member_row(r)
    h, c = member_row(c)
    pair = jnp.where(g < n_row, 0, 1)
    row_ids = ((g - pair * n_row) * (2 * n_t) + plane * 2 + pair) * rows + r
    col_ids = ((h * 2 + core) * n_row + row) * rows + c
    label = jnp.where(row_ids == col_ids, F32(1.0), F32(-1.0))
    margin = label * (temperature * scores + bias_ref[...])
    weights = -label * jax.nn.sigmoid(-margin)
    wt[...] = weights.T.astype(BF16)
    w[...] = weights.astype(BF16)

    to_blocks(jnp.dot(wt[...], images, preferred_element_type=F32), pt)
    if line:
        end = jnp.logical_or(first_end, last_end)
        opposite = jnp.where(first_end, 3, 0)
        push(pt.at[opposite], rl, pair_sem.at[1], at_plane(jnp.where(first_end, 1, 2)), end)
        through = jnp.logical_not(relay)
    for k in order:
        push(pt.at[planes[k]], rt.at[plane], ct2.at[plane], at_plane(planes[k]),
             through if line and k == 2 else direct(k))

    def half(c):
        some = w[pl.ds(pl.multiple_of(c * (24 * n_row), 16), 24 * n_row)]
        return jnp.dot(some, texts, preferred_element_type=F32)

    to_blocks(half(other_core), ps)
    push(ps, rs, pair_sem.at[0], sibling)
    to_blocks(half(core), po)
    arrived(rs, pair_sem.at[0])
    for r in other_rows:
        pi[r] = (po[r] + rs[r].astype(F32)).astype(BF16)
        push(pi.at[r], ri.at[row], ci2.at[row], at_row(r))
    if line:
        @pl.when(relay)
        def _():
            arrived(rl, pair_sem.at[1])
            pt[far_end] = (pt[far_end].astype(F32) + rl[...].astype(F32)).astype(BF16)
        push(pt.at[far_end], rt.at[plane], ct2.at[plane], at_plane(far_end), relay)

    def rows_of(total):
        return temperature * jnp.concatenate([total[:, :width], unpack_tail(total[:, width:], width)], axis=0)

    acc[...] = po[row] + rs[row].astype(F32)
    for r in other_rows:
        arrived(ri.at[r], ci2.at[r])
        acc[...] += ri[r].astype(F32)
    oi[...] = norm_back(iu[pl.ds(pl.multiple_of(me_i * 24, 8), 24)], il[:, :1], rows_of(acc[...]))[:rows]
    out_i = pltpu.make_async_copy(oi, gimg_ref, out_sem.at[0])
    out_i.start()
    acc[...] = pt[plane].astype(F32)
    for k in order[1:] + order[:1]:
        h = planes[k]

        def add(h=h):
            arrived(rt.at[h], ct2.at[h])
            acc[...] += rt[h].astype(F32)

        when(direct(k))(add)
    ot[...] = norm_back(tu[pl.ds(pl.multiple_of(plane * 24, 8), 24)], tl[:, :1], rows_of(acc[...]))[:rows]
    out_t = pltpu.make_async_copy(ot, gtxt_ref, out_sem.at[1])
    out_t.start()
    for copy, condition in sent:
        when(condition)(lambda copy=copy: copy().wait_send())
    out_i.wait()
    out_t.wait()


def hand_over(gimg_ref, gtxt_ref, images_ref, texts_ref, sem):
    copies = [pltpu.make_async_copy(gimg_ref, images_ref, sem.at[0]),
              pltpu.make_async_copy(gtxt_ref, texts_ref, sem.at[1])]
    for copy in copies:
        copy.start()
    for copy in copies:
        copy.wait()


def on_device(n_row, n_col, images, texts, logarithmic_scale, similarity_bias):
    rows, width = images.shape
    pad = 24
    packed = width + -(-width // 256) * 128
    assert 16 < rows <= pad and n_col % 2 == 0 and n_row % 2 == 0
    n_i, n_t = 2 * n_row, n_col // 2
    hbm = pl.BlockSpec(memory_space=pl.ANY)
    smem = pl.BlockSpec(memory_space=pltpu.SMEM)
    out = jax.ShapeDtypeStruct((rows, width), F32)
    dma = pltpu.SemaphoreType.DMA

    def blocks(n, kind=BF16):
        return pltpu.VMEM((n, 16, packed), kind)

    grads = pl.pallas_call(
        functools.partial(kernel, n_row, n_t),
        out_shape=(out, out),
        in_specs=[hbm, hbm, smem, smem],
        out_specs=(hbm, hbm),
        scratch_shapes=[
            pltpu.VMEM((rows, width), F32),
            pltpu.VMEM((rows, width), F32),
            pltpu.VMEM((n_i * pad, width), F32),
            pltpu.VMEM((n_t * pad, width), F32),
            pltpu.VMEM((pad, 128), F32),
            pltpu.VMEM((pad, 128), F32),
            pltpu.VMEM((n_i, rows, width), BF16),
            pltpu.VMEM((n_t, rows, width), BF16),
            pltpu.VMEM((n_t * pad, n_i * pad), BF16),
            pltpu.VMEM((n_i * pad, n_t * pad), BF16),
            blocks(n_t),
            blocks(n_row),
            blocks(n_row, F32),
            blocks(n_row),
            pltpu.VMEM((16, packed), F32),
            blocks(n_t),
            pltpu.VMEM((16, packed), BF16),
            blocks(n_row),
            blocks(n_row),
            dma((2,)), dma((2,)), dma((3 * n_row + 2 * n_t + 2,)),
            dma((n_i,)), dma((n_t,)), dma((n_t,)), dma((n_row,)), dma((2,)),
        ],
        compiler_params=pltpu.CompilerParams(
            collective_id=0, has_side_effects=True),
    )(images, texts, logarithmic_scale, similarity_bias)
    return pl.pallas_call(
        hand_over,
        out_shape=(out, out),
        in_specs=[hbm, hbm],
        out_specs=(hbm, hbm),
        scratch_shapes=[dma((2,))],
    )(*grads)


def solution(mesh):
    return jax.shard_map(
        functools.partial(on_device, mesh.shape["row"], mesh.shape["col"]),
        mesh=mesh,
        in_specs=(P(("row", "col"), None), P(("col", "row"), None), P(), P()),
        out_specs=(P(("row", "col"), None), P(("col", "row"), None)),
        check_vma=False,
    )
```

```python
import functools

import jax
import jax.numpy as jnp
from jax import lax
from jax.experimental import pallas as pl
from jax.experimental.pallas import tpu as pltpu
from jax.sharding import PartitionSpec as P

MESH = pl.DeviceIdType.MESH
F32, BF16 = jnp.float32, jnp.bfloat16


def pack(x):
    width = x.shape[1]
    left = -(-width // 256) * 128
    right = jnp.concatenate([x[16:, left:], jnp.zeros((8, 2 * left - width), x.dtype)], axis=1)
    return x[:16], jnp.concatenate([x[16:, :left], right], axis=0)


def unpack_tail(tail, width):
    left = tail.shape[1]
    return jnp.concatenate([tail[:8], tail[8:, :width - left]], axis=1)


def unit_rows(x_ref, wide, length_ref, unit_ref, block_ref):
    rows, width = x_ref.shape
    wide[...] = jnp.zeros_like(wide)
    wide[:rows] = x_ref[...].astype(F32)
    x = wide[...]
    length = jnp.sqrt(jnp.sum(x * x, axis=1, keepdims=True) + 1e-06)
    unit = x / length
    unit_ref[...] = unit
    length_ref[...] = jnp.broadcast_to(length, length_ref.shape)
    head, tail = pack(unit)
    block_ref[:, :width] = head.astype(BF16)
    block_ref[:, width:] = tail.astype(BF16)


def all_rows(blocks, width):
    n = blocks.shape[0]
    heads = blocks[:, :, :width].reshape(n * 16, width)
    tails = [unpack_tail(blocks[k, :, width:].astype(F32), width) for k in range(n)]
    return jnp.concatenate([heads, jnp.concatenate(tails, axis=0).astype(BF16)], axis=0)


def to_blocks(partial, blocks):
    n, width = blocks.shape[0], partial.shape[1]
    for k in range(n):
        head, tail = pack(jnp.concatenate(
            [partial[16 * k:16 * k + 16], partial[16 * n + 8 * k:16 * n + 8 * k + 8]], axis=0))
        blocks[k, :, :width] = head.astype(blocks.dtype)
        blocks[k, :, width:] = tail.astype(blocks.dtype)


def member_row(index, n):
    tail = index - 16 * n
    member = jnp.where(index < 16 * n, index // 16, tail // 8)
    return member, jnp.where(index < 16 * n, index % 16, 16 + tail % 8)


def norm_back(unit, length, upstream):
    along = jnp.sum(unit * upstream, axis=1, keepdims=True)
    return (upstream - unit * along) / length


def kernel(n_row, n_t, img_ref, txt_ref, scale_ref, bias_ref, gimg_ref, gtxt_ref,
           xi, xt, wide, iu, tu, il, tl, gi, gt, label_ref, wt, wh, wl, pt, ps, po, pi, acc, rt, rs, ri,
           in_sem, send_sem, ci, ct, ct2, ci2, pair_sem):
    rows, width = img_ref.shape
    load_t = pltpu.make_async_copy(txt_ref, xt, in_sem.at[0])
    load_i = pltpu.make_async_copy(img_ref, xi, in_sem.at[1])
    load_t.start()
    load_i.start()
    n_i = 2 * n_row
    row, col = lax.axis_index("row"), lax.axis_index("col")
    plane, core = col // 2, col % 2
    other_core = 1 - core
    me_i = core * n_row + row
    low = plane < n_t // 2
    from_end = jnp.where(low, plane, n_t - 1 - plane)
    planes = []
    for t in range(n_t - 1, 0, -1):
        t = jnp.where(t > from_end, t, t - 1)
        planes.append(jnp.where(low, t, n_t - 1 - t))

    def at_row(r):
        return (r, col)

    def at_plane(h):
        return (row, 2 * h + core)

    sibling = (row, 2 * plane + other_core)
    other_rows = [lax.rem(row + k, n_row) for k in range(1, n_row)]

    barrier = pltpu.get_barrier_semaphore()
    for place in [at_plane(h) for h in planes] + [at_row(r) for r in other_rows] + [sibling]:
        pl.semaphore_signal(barrier, inc=1, device_id=place, device_id_type=MESH)
    load_t.wait()
    unit_rows(xt, wide, tl, tu, gt.at[plane])
    load_i.wait()
    unit_rows(xi, wide, il, iu, gi.at[me_i])
    r = lax.broadcasted_iota(jnp.int32, (24 * n_i, 1), 0)
    c = lax.broadcasted_iota(jnp.int32, (1, 24 * n_t), 1)
    g, r = member_row(r, n_i)
    h, c = member_row(c, n_t)
    row_ids = ((g % n_row) * (2 * n_t) + plane * 2 + g // n_row) * rows + r
    col_ids = ((h * 2 + core) * n_row + row) * rows + c
    label = jnp.where(row_ids == col_ids, F32(1.0), F32(-1.0))
    label_ref[...] = label
    temperature = jnp.exp(jnp.full((1, 1), scale_ref[...], F32))
    pl.semaphore_wait(barrier, n_row + n_t - 1)

    sent = []

    def push(src, dst, recv, place):
        copy = pltpu.make_async_remote_copy(
            src_ref=src, dst_ref=dst, send_sem=send_sem.at[len(sent)], recv_sem=recv,
            device_id=place, device_id_type=MESH)
        copy.start()
        sent.append(copy)

    def arrived(dst, recv):
        pltpu.make_async_remote_copy(
            src_ref=dst, dst_ref=dst, send_sem=send_sem.at[0], recv_sem=recv,
            device_id=sibling, device_id_type=MESH).wait_recv()

    for h in planes:
        push(gt.at[plane], gt.at[plane], ct.at[plane], at_plane(h))
    for r in other_rows:
        push(gi.at[me_i], gi.at[me_i], ci.at[me_i], at_row(r))
    push(gi.at[me_i], gi.at[me_i], ci.at[me_i], sibling)
    for r in other_rows:
        g = core * n_row + r
        arrived(gi.at[g], ci.at[g])
        push(gi.at[g], gi.at[g], ci.at[g], sibling)
    for r in [row] + other_rows:
        g = other_core * n_row + r
        arrived(gi.at[g], ci.at[g])
    images = all_rows(gi, width)
    for h in planes[::-1]:
        arrived(gt.at[h], ct.at[h])
    texts = all_rows(gt, width)
    scores = lax.dot_general(images, texts, (((1,), (1,)), ((), ())), preferred_element_type=F32)
    label = label_ref[...]
    margin = label * (temperature * scores + bias_ref[...])
    weights = -label * jax.nn.sigmoid(-margin)
    wt[...] = weights.T.astype(BF16)
    wh[...] = weights[:16 * n_i].astype(BF16)
    wl[...] = weights[16 * n_i:].astype(BF16)

    to_blocks(jnp.dot(wt[...], images, preferred_element_type=F32), pt)
    for h in planes:
        push(pt.at[h], rt.at[plane], ct2.at[plane], at_plane(h))

    def half(c):
        head = wh[pl.ds(pl.multiple_of(c * (16 * n_row), 16), 16 * n_row)]
        tail = wl[pl.ds(pl.multiple_of(c * (8 * n_row), 16), 8 * n_row)]
        return jnp.dot(jnp.concatenate([head, tail], axis=0), texts, preferred_element_type=F32)

    to_blocks(half(other_core), ps)
    push(ps, rs, pair_sem.at[0], sibling)
    to_blocks(half(core), po)
    arrived(rs, pair_sem.at[0])
    for r in other_rows:
        pi[r] = (po[r] + rs[r].astype(F32)).astype(BF16)
        push(pi.at[r], ri.at[row], ci2.at[row], at_row(r))

    def rows_of(total):
        return temperature * jnp.concatenate([total[:, :width], unpack_tail(total[:, width:], width)], axis=0)

    acc[...] = po[row] + rs[row].astype(F32)
    for r in other_rows:
        arrived(ri.at[r], ci2.at[r])
        acc[...] += ri[r].astype(F32)
    gimg_ref[...] = norm_back(iu[...], il[:, :1], rows_of(acc[...]))[:rows]
    acc[...] = pt[plane].astype(F32)
    for h in planes[::-1]:
        arrived(rt.at[h], ct2.at[h])
        acc[...] += rt[h].astype(F32)
    gtxt_ref[...] = norm_back(tu[...], tl[:, :1], rows_of(acc[...]))[:rows]
    for copy in sent:
        copy.wait_send()


def hand_over(gimg_ref, gtxt_ref, images_ref, texts_ref):
    images_ref[...] = gimg_ref[...]
    texts_ref[...] = gtxt_ref[...]


def on_device(n_row, n_col, images, texts, logarithmic_scale, similarity_bias):
    rows, width = images.shape
    pad = 24
    packed = width + -(-width // 256) * 128
    assert 16 < rows <= pad and n_col % 2 == 0 and n_row % 2 == 0
    n_i, n_t = 2 * n_row, n_col // 2
    vmem = pl.BlockSpec(memory_space=pltpu.VMEM)
    hbm = pl.BlockSpec(memory_space=pltpu.HBM)
    smem = pl.BlockSpec(memory_space=pltpu.SMEM)
    out = jax.ShapeDtypeStruct((rows, width), F32)
    dma = pltpu.SemaphoreType.DMA

    def blocks(n, kind=BF16):
        return pltpu.VMEM((n, 16, packed), kind)

    grads = pl.pallas_call(
        functools.partial(kernel, n_row, n_t),
        out_shape=(out, out),
        in_specs=[hbm, hbm, smem, smem],
        out_specs=(vmem, vmem),
        scratch_shapes=[
            pltpu.VMEM((rows, width), BF16),
            pltpu.VMEM((rows, width), BF16),
            pltpu.VMEM((pad, width), F32),
            pltpu.VMEM((pad, width), F32),
            pltpu.VMEM((pad, width), F32),
            pltpu.VMEM((pad, 128), F32),
            pltpu.VMEM((pad, 128), F32),
            blocks(n_i),
            blocks(n_t),
            pltpu.VMEM((n_i * pad, n_t * pad), F32),
            pltpu.VMEM((n_t * pad, n_i * pad), BF16),
            pltpu.VMEM((n_i * 16, n_t * pad), BF16),
            pltpu.VMEM((n_i * 8, n_t * pad), BF16),
            blocks(n_t),
            blocks(n_row),
            blocks(n_row, F32),
            blocks(n_row),
            pltpu.VMEM((16, packed), F32),
            blocks(n_t),
            blocks(n_row),
            blocks(n_row),
            dma((2,)), dma((3 * n_row + 2 * n_t + 2,)),
            dma((n_i,)), dma((n_t,)), dma((n_t,)), dma((n_row,)), dma((1,)),
        ],
        compiler_params=pltpu.CompilerParams(
            collective_id=0, has_side_effects=True),
    )(images, texts, logarithmic_scale, similarity_bias)
    return pl.pallas_call(
        hand_over, out_shape=(out, out), in_specs=[vmem, vmem], out_specs=(vmem, vmem))(*grads)


def solution(mesh):
    return jax.shard_map(
        functools.partial(on_device, mesh.shape["row"], mesh.shape["col"]),
        mesh=mesh,
        in_specs=(P(("row", "col"), None), P(("col", "row"), None), P(), P()),
        out_specs=(P(("row", "col"), None), P(("col", "row"), None)),
        check_vma=False,
    )
```

```python
import functools

import jax
import jax.numpy as jnp
from jax import lax
from jax.experimental import pallas as pl
from jax.experimental.pallas import tpu as pltpu
from jax.sharding import PartitionSpec as P

MESH = pl.DeviceIdType.MESH
F32, BF16 = jnp.float32, jnp.bfloat16


def pack(x):
    width = x.shape[1]
    left = -(-width // 256) * 128
    right = jnp.concatenate([x[16:, left:], jnp.zeros((8, 2 * left - width), x.dtype)], axis=1)
    return x[:16], jnp.concatenate([x[16:, :left], right], axis=0)


def unpack_tail(tail, width):
    left = tail.shape[1]
    return jnp.concatenate([tail[:8], tail[8:, :width - left]], axis=1)


def unit_rows(x_ref, wide, length_ref, unit_ref, block_ref):
    rows, width = x_ref.shape
    wide[...] = jnp.zeros_like(wide)
    wide[:rows] = x_ref[...].astype(F32)
    x = wide[...]
    length = jnp.sqrt(jnp.sum(x * x, axis=1, keepdims=True) + 1e-06)
    unit = x / length
    unit_ref[...] = unit
    length_ref[...] = jnp.broadcast_to(length, length_ref.shape)
    head, tail = pack(unit)
    block_ref[:, :width] = head.astype(BF16)
    block_ref[:, width:] = tail.astype(BF16)


def all_rows(blocks, width):
    n = blocks.shape[0]
    heads = blocks[:, :, :width].reshape(n * 16, width)
    tails = [unpack_tail(blocks[k, :, width:].astype(F32), width) for k in range(n)]
    return jnp.concatenate([heads, jnp.concatenate(tails, axis=0).astype(BF16)], axis=0)


def to_blocks(partial, blocks):
    n, width = blocks.shape[0], partial.shape[1]
    for k in range(n):
        head, tail = pack(jnp.concatenate(
            [partial[16 * k:16 * k + 16], partial[16 * n + 8 * k:16 * n + 8 * k + 8]], axis=0))
        blocks[k, :, :width] = head.astype(blocks.dtype)
        blocks[k, :, width:] = tail.astype(blocks.dtype)


def member_row(index, n):
    tail = index - 16 * n
    member = jnp.where(index < 16 * n, index // 16, tail // 8)
    return member, jnp.where(index < 16 * n, index % 16, 16 + tail % 8)


def norm_back(unit, length, upstream):
    along = jnp.sum(unit * upstream, axis=1, keepdims=True)
    return (upstream - unit * along) / length


def kernel(n_row, n_t, img_ref, txt_ref, scale_ref, bias_ref, gimg_ref, gtxt_ref,
           xi, xt, wide, iu, tu, il, tl, gi, gt, label_ref, im, tx, wt, wh, wl, pt, ps, po, pi, acc, rt, rs, ri,
           in_sem, send_sem, ci, ct, ct2, ci2, pair_sem):
    rows, width = img_ref.shape
    load_t = pltpu.make_async_copy(txt_ref, xt, in_sem.at[0])
    load_i = pltpu.make_async_copy(img_ref, xi, in_sem.at[1])
    load_t.start()
    load_i.start()
    n_i = 2 * n_row
    row, col = lax.axis_index("row"), lax.axis_index("col")
    plane, core = col // 2, col % 2
    other_core = 1 - core
    me_i = core * n_row + row
    low = plane < n_t // 2
    from_end = jnp.where(low, plane, n_t - 1 - plane)
    planes = []
    for t in range(n_t - 1, 0, -1):
        t = jnp.where(t > from_end, t, t - 1)
        planes.append(jnp.where(low, t, n_t - 1 - t))

    def at_row(r):
        return (r, col)

    def at_plane(h):
        return (row, 2 * h + core)

    sibling = (row, 2 * plane + other_core)
    other_rows = [lax.rem(row + k, n_row) for k in range(1, n_row)]

    barrier = pltpu.get_barrier_semaphore()
    for place in [at_plane(h) for h in planes] + [at_row(r) for r in other_rows] + [sibling]:
        pl.semaphore_signal(barrier, inc=1, device_id=place, device_id_type=MESH)
    load_t.wait()
    unit_rows(xt, wide, tl, tu, gt.at[plane])
    load_i.wait()
    unit_rows(xi, wide, il, iu, gi.at[me_i])
    h_n = n_t // 2
    slab = 24 * h_n
    g, r = member_row(lax.broadcasted_iota(jnp.int32, (1, 24 * n_i), 1), n_i)
    row_ids = ((g % n_row) * (2 * n_t) + plane * 2 + g // n_row) * rows + r
    h, c = member_row(lax.broadcasted_iota(jnp.int32, (slab, 1), 0), h_n)
    for q in range(2):
        col_ids = (((h + q * h_n) * 2 + core) * n_row + row) * rows + c
        label_ref[q * slab:(q + 1) * slab] = jnp.where(row_ids == col_ids, F32(1.0), F32(-1.0))
    temperature = jnp.exp(jnp.full((1, 1), scale_ref[...], F32))
    pl.semaphore_wait(barrier, n_row + n_t - 1)

    sent = []

    def push(src, dst, recv, place):
        copy = pltpu.make_async_remote_copy(
            src_ref=src, dst_ref=dst, send_sem=send_sem.at[len(sent)], recv_sem=recv,
            device_id=place, device_id_type=MESH)
        copy.start()
        sent.append((copy, None))

    def arrived(dst, recv):
        pltpu.make_async_remote_copy(
            src_ref=dst, dst_ref=dst, send_sem=send_sem.at[0], recv_sem=recv,
            device_id=sibling, device_id_type=MESH).wait_recv()

    for h in planes:
        push(gt.at[plane], gt.at[plane], ct.at[plane], at_plane(h))
    for r in other_rows:
        push(gi.at[me_i], gi.at[me_i], ci.at[me_i], at_row(r))
    push(gi.at[me_i], gi.at[me_i], ci.at[me_i], sibling)
    for r in other_rows:
        g = core * n_row + r
        arrived(gi.at[g], ci.at[g])
        push(gi.at[g], gi.at[g], ci.at[g], sibling)
    for r in [row] + other_rows:
        g = other_core * n_row + r
        arrived(gi.at[g], ci.at[g])
    im[...] = all_rows(gi[...], width)

    mine = plane // h_n
    first = jnp.where(from_end < (h_n + 1) // 2, 1 - mine, mine)
    for q in (first, 1 - first):
        for j in range(h_n):
            h = q * h_n + j

            @pl.when(h != plane)
            def _():
                arrived(gt.at[h], ct.at[h])

        at = pl.ds(pl.multiple_of(q * slab, 16), slab)
        tx[at] = all_rows(gt[pl.ds(q * h_n, h_n)], width)
        scores = lax.dot_general(tx[at], im[...], (((1,), (1,)), ((), ())), preferred_element_type=F32)
        label = label_ref[at]
        margin = label * (temperature * scores + bias_ref[...])
        wt[at] = (-label * jax.nn.sigmoid(-margin)).astype(BF16)
        to_blocks(jnp.dot(wt[at], im[...], preferred_element_type=F32), pt.at[pl.ds(q * h_n, h_n)])
        for j in range(h_n):
            h = q * h_n + j
            slot = send_sem.at[len(sent)]
            copy = pltpu.make_async_remote_copy(
                src_ref=pt.at[h], dst_ref=rt.at[plane], send_sem=slot, recv_sem=ct2.at[plane],
                device_id=at_plane(h), device_id_type=MESH)

            @pl.when(h != plane)
            def _():
                copy.start()

            sent.append((copy, h != plane))

    w = wt[...].astype(F32).T.astype(BF16)
    wh[...] = w[:16 * n_i]
    wl[...] = w[16 * n_i:]

    def half(c):
        head = wh[pl.ds(pl.multiple_of(c * (16 * n_row), 16), 16 * n_row)]
        tail = wl[pl.ds(pl.multiple_of(c * (8 * n_row), 16), 8 * n_row)]
        return jnp.dot(jnp.concatenate([head, tail], axis=0), tx[...], preferred_element_type=F32)

    to_blocks(half(other_core), ps)
    push(ps, rs, pair_sem.at[0], sibling)
    to_blocks(half(core), po)
    arrived(rs, pair_sem.at[0])
    for r in other_rows:
        pi[r] = (po[r] + rs[r].astype(F32)).astype(BF16)
        push(pi.at[r], ri.at[row], ci2.at[row], at_row(r))

    def rows_of(total):
        return temperature * jnp.concatenate([total[:, :width], unpack_tail(total[:, width:], width)], axis=0)

    acc[...] = pt[plane].astype(F32)
    for h in planes[::-1]:
        arrived(rt.at[h], ct2.at[h])
        acc[...] += rt[h].astype(F32)
    gtxt_ref[...] = norm_back(tu[...], tl[:, :1], rows_of(acc[...]))[:rows]
    acc[...] = po[row] + rs[row].astype(F32)
    for r in other_rows:
        arrived(ri.at[r], ci2.at[r])
        acc[...] += ri[r].astype(F32)
    gimg_ref[...] = norm_back(iu[...], il[:, :1], rows_of(acc[...]))[:rows]
    for copy, condition in sent:
        if condition is None:
            copy.wait_send()
        else:
            pl.when(condition)(copy.wait_send)


def hand_over(gimg_ref, gtxt_ref, images_ref, texts_ref):
    images_ref[...] = gimg_ref[...]
    texts_ref[...] = gtxt_ref[...]


def on_device(n_row, n_col, images, texts, logarithmic_scale, similarity_bias):
    rows, width = images.shape
    pad = 24
    packed = width + -(-width // 256) * 128
    assert 16 < rows <= pad and n_col % 8 == 0 and n_row % 2 == 0
    n_i, n_t = 2 * n_row, n_col // 2
    vmem = pl.BlockSpec(memory_space=pltpu.VMEM)
    hbm = pl.BlockSpec(memory_space=pltpu.HBM)
    smem = pl.BlockSpec(memory_space=pltpu.SMEM)
    out = jax.ShapeDtypeStruct((rows, width), F32)
    dma = pltpu.SemaphoreType.DMA

    def blocks(n, kind=BF16):
        return pltpu.VMEM((n, 16, packed), kind)

    grads = pl.pallas_call(
        functools.partial(kernel, n_row, n_t),
        out_shape=(out, out),
        in_specs=[hbm, hbm, smem, smem],
        out_specs=(vmem, vmem),
        scratch_shapes=[
            pltpu.VMEM((rows, width), BF16),
            pltpu.VMEM((rows, width), BF16),
            pltpu.VMEM((pad, width), F32),
            pltpu.VMEM((pad, width), F32),
            pltpu.VMEM((pad, width), F32),
            pltpu.VMEM((pad, 128), F32),
            pltpu.VMEM((pad, 128), F32),
            blocks(n_i),
            blocks(n_t),
            pltpu.VMEM((n_t * pad, n_i * pad), F32),
            pltpu.VMEM((n_i * pad, width), BF16),
            pltpu.VMEM((n_t * pad, width), BF16),
            pltpu.VMEM((n_t * pad, n_i * pad), BF16),
            pltpu.VMEM((n_i * 16, n_t * pad), BF16),
            pltpu.VMEM((n_i * 8, n_t * pad), BF16),
            blocks(n_t),
            blocks(n_row),
            blocks(n_row, F32),
            blocks(n_row),
            pltpu.VMEM((16, packed), F32),
            blocks(n_t),
            blocks(n_row),
            blocks(n_row),
            dma((2,)), dma((3 * n_row + 2 * n_t + 4,)),
            dma((n_i,)), dma((n_t,)), dma((n_t,)), dma((n_row,)), dma((1,)),
        ],
        compiler_params=pltpu.CompilerParams(
            collective_id=0, has_side_effects=True),
    )(images, texts, logarithmic_scale, similarity_bias)
    return pl.pallas_call(
        hand_over, out_shape=(out, out), in_specs=[vmem, vmem], out_specs=(vmem, vmem))(*grads)


def solution(mesh):
    return jax.shard_map(
        functools.partial(on_device, mesh.shape["row"], mesh.shape["col"]),
        mesh=mesh,
        in_specs=(P(("row", "col"), None), P(("col", "row"), None), P(), P()),
        out_specs=(P(("row", "col"), None), P(("col", "row"), None)),
        check_vma=False,
    )
```

```python
import functools

import jax
import jax.numpy as jnp
from jax import lax
from jax.experimental import pallas as pl
from jax.experimental.pallas import tpu as pltpu
from jax.sharding import PartitionSpec as P

MESH = pl.DeviceIdType.MESH
F32, BF16 = jnp.float32, jnp.bfloat16


def pack(x):
    width = x.shape[1]
    left = -(-width // 256) * 128
    right = jnp.concatenate([x[16:, left:], jnp.zeros((8, 2 * left - width), x.dtype)], axis=1)
    return x[:16], jnp.concatenate([x[16:, :left], right], axis=0)


def unpack_tail(tail, width):
    left = tail.shape[1]
    return jnp.concatenate([tail[:8], tail[8:, :width - left]], axis=1)


def unit_rows(x_ref, wide, length_ref, unit_ref, block_ref):
    rows, width = x_ref.shape
    wide[...] = jnp.zeros_like(wide)
    wide[:rows] = x_ref[...].astype(F32)
    x = wide[...]
    length = jnp.sqrt(jnp.sum(x * x, axis=1, keepdims=True) + 1e-06)
    unit = x / length
    unit_ref[...] = unit
    length_ref[...] = jnp.broadcast_to(length, length_ref.shape)
    head, tail = pack(unit)
    block_ref[:, :width] = head.astype(BF16)
    block_ref[:, width:] = tail.astype(BF16)


def all_rows(blocks, width):
    n = blocks.shape[0]
    heads = blocks[:, :, :width].reshape(n * 16, width)
    tails = [unpack_tail(blocks[k, :, width:].astype(F32), width) for k in range(n)]
    return jnp.concatenate([heads, jnp.concatenate(tails, axis=0).astype(BF16)], axis=0)


def to_blocks(partial, blocks):
    n, width = blocks.shape[0], partial.shape[1]
    for k in range(n):
        head, tail = pack(jnp.concatenate(
            [partial[16 * k:16 * k + 16], partial[16 * n + 8 * k:16 * n + 8 * k + 8]], axis=0))
        blocks[k, :, :width] = head.astype(blocks.dtype)
        blocks[k, :, width:] = tail.astype(blocks.dtype)


def member_row(index, n):
    tail = index - 16 * n
    member = jnp.where(index < 16 * n, index // 16, tail // 8)
    return member, jnp.where(index < 16 * n, index % 16, 16 + tail % 8)


def norm_back(unit, length, upstream):
    along = jnp.sum(unit * upstream, axis=1, keepdims=True)
    return (upstream - unit * along) / length


def kernel(n_row, n_t, img_ref, txt_ref, scale_ref, bias_ref, gimg_ref, gtxt_ref,
           xi, xt, wide, iu, tu, il, tl, gi, gt, label_ref, wt, wh, wl, pt, ps, po, pi, acc, rt, rs, ri,
           in_sem, line_sem, send_sem, ci, ct, ct2, ci2, pair_sem):
    rows, width = img_ref.shape
    load_t = pltpu.make_async_copy(txt_ref, xt, in_sem.at[0])
    load_i = pltpu.make_async_copy(img_ref, xi, in_sem.at[1])
    load_t.start()
    load_i.start()
    n_i = 2 * n_row
    row, col = lax.axis_index("row"), lax.axis_index("col")
    plane, core = col // 2, col % 2
    other_core = 1 - core
    me_i = core * n_row + row
    low = plane < n_t // 2
    from_end = jnp.where(low, plane, n_t - 1 - plane)
    planes = []
    for t in range(n_t - 1, 0, -1):
        t = jnp.where(t > from_end, t, t - 1)
        planes.append(jnp.where(low, t, n_t - 1 - t))

    line = n_t == 4
    is_end, is_relay = from_end == 0, from_end == 1
    far_end, near_end = jnp.where(low, 3, 0), jnp.where(low, 0, 3)

    def at_row(r):
        return (r, col)

    def at_plane(h):
        return (row, 2 * h + core)

    sibling = (row, 2 * plane + other_core)
    other_rows = [lax.rem(row + k, n_row) for k in range(1, n_row)]

    barrier = pltpu.get_barrier_semaphore()
    for place in [at_plane(h) for h in planes] + [at_row(r) for r in other_rows] + [sibling]:
        pl.semaphore_signal(barrier, inc=1, device_id=place, device_id_type=MESH)
    load_t.wait()
    unit_rows(xt, wide, tl, tu, gt.at[plane])
    load_i.wait()
    unit_rows(xi, wide, il, iu, gi.at[me_i])
    r = lax.broadcasted_iota(jnp.int32, (24 * n_i, 1), 0)
    c = lax.broadcasted_iota(jnp.int32, (1, 24 * n_t), 1)
    g, r = member_row(r, n_i)
    h, c = member_row(c, n_t)
    row_ids = ((g % n_row) * (2 * n_t) + plane * 2 + g // n_row) * rows + r
    col_ids = ((h * 2 + core) * n_row + row) * rows + c
    label = jnp.where(row_ids == col_ids, F32(1.0), F32(-1.0))
    label_ref[...] = label
    temperature = jnp.exp(jnp.full((1, 1), scale_ref[...], F32))
    pl.semaphore_wait(barrier, n_row + n_t - 1)

    sent = []

    def push(src, dst, recv, place):
        copy = pltpu.make_async_remote_copy(
            src_ref=src, dst_ref=dst, send_sem=send_sem.at[len(sent)], recv_sem=recv,
            device_id=place, device_id_type=MESH)
        copy.start()
        sent.append(copy)

    def arrived(dst, recv):
        pltpu.make_async_remote_copy(
            src_ref=dst, dst_ref=dst, send_sem=send_sem.at[0], recv_sem=recv,
            device_id=sibling, device_id_type=MESH).wait_recv()

    def text_copy(block, h, slot):
        return pltpu.make_async_remote_copy(
            src_ref=gt.at[block], dst_ref=gt.at[block], send_sem=line_sem.at[slot],
            recv_sem=ct.at[block], device_id=at_plane(h), device_id_type=MESH)

    if line:
        across, inner, near = planes[0], planes[1], planes[2]
        text_copy(plane, inner, 1).start()

        @pl.when(is_relay)
        def _():
            text_copy(plane, across, 0).start()

        text_copy(plane, near, 2).start()
    else:
        for h in planes:
            push(gt.at[plane], gt.at[plane], ct.at[plane], at_plane(h))
    for r in other_rows:
        push(gi.at[me_i], gi.at[me_i], ci.at[me_i], at_row(r))
    push(gi.at[me_i], gi.at[me_i], ci.at[me_i], sibling)
    for k, r in enumerate(other_rows):
        g = core * n_row + r
        arrived(gi.at[g], ci.at[g])
        push(gi.at[g], gi.at[g], ci.at[g], sibling)
        if line and k == 0:
            @pl.when(is_relay)
            def _():
                arrived(gt.at[far_end], ct.at[far_end])
                text_copy(far_end, near_end, 3).start()
    for r in [row] + other_rows:
        g = other_core * n_row + r
        arrived(gi.at[g], ci.at[g])
    images = all_rows(gi, width)
    if line:
        arrived(gt.at[near], ct.at[near])
        arrived(gt.at[inner], ct.at[inner])

        @pl.when(is_end)
        def _():
            arrived(gt.at[far_end], ct.at[far_end])
    else:
        for h in planes[::-1]:
            arrived(gt.at[h], ct.at[h])
    texts = all_rows(gt, width)
    scores = lax.dot_general(images, texts, (((1,), (1,)), ((), ())), preferred_element_type=F32)
    label = label_ref[...]
    margin = label * (temperature * scores + bias_ref[...])
    weights = -label * jax.nn.sigmoid(-margin)
    wt[...] = weights.T.astype(BF16)
    wh[...] = weights[:16 * n_i].astype(BF16)
    wl[...] = weights[16 * n_i:].astype(BF16)

    to_blocks(jnp.dot(wt[...], images, preferred_element_type=F32), pt)
    for h in planes:
        push(pt.at[h], rt.at[plane], ct2.at[plane], at_plane(h))

    def half(c):
        head = wh[pl.ds(pl.multiple_of(c * (16 * n_row), 16), 16 * n_row)]
        tail = wl[pl.ds(pl.multiple_of(c * (8 * n_row), 16), 8 * n_row)]
        return jnp.dot(jnp.concatenate([head, tail], axis=0), texts, preferred_element_type=F32)

    to_blocks(half(other_core), ps)
    push(ps, rs, pair_sem.at[0], sibling)
    to_blocks(half(core), po)
    arrived(rs, pair_sem.at[0])
    for r in other_rows:
        pi[r] = (po[r] + rs[r].astype(F32)).astype(BF16)
        push(pi.at[r], ri.at[row], ci2.at[row], at_row(r))

    def rows_of(total):
        return temperature * jnp.concatenate([total[:, :width], unpack_tail(total[:, width:], width)], axis=0)

    acc[...] = po[row] + rs[row].astype(F32)
    for r in other_rows:
        arrived(ri.at[r], ci2.at[r])
        acc[...] += ri[r].astype(F32)
    gimg_ref[...] = norm_back(iu[...], il[:, :1], rows_of(acc[...]))[:rows]
    acc[...] = pt[plane].astype(F32)
    for h in planes[::-1]:
        arrived(rt.at[h], ct2.at[h])
        acc[...] += rt[h].astype(F32)
    gtxt_ref[...] = norm_back(tu[...], tl[:, :1], rows_of(acc[...]))[:rows]
    for copy in sent:
        copy.wait_send()
    if line:
        text_copy(plane, inner, 1).wait_send()
        text_copy(plane, near, 2).wait_send()

        @pl.when(is_relay)
        def _():
            text_copy(plane, across, 0).wait_send()
            text_copy(far_end, near_end, 3).wait_send()


def hand_over(gimg_ref, gtxt_ref, images_ref, texts_ref):
    images_ref[...] = gimg_ref[...]
    texts_ref[...] = gtxt_ref[...]


def on_device(n_row, n_col, images, texts, logarithmic_scale, similarity_bias):
    rows, width = images.shape
    pad = 24
    packed = width + -(-width // 256) * 128
    assert 16 < rows <= pad and n_col % 2 == 0 and n_row % 2 == 0
    n_i, n_t = 2 * n_row, n_col // 2
    vmem = pl.BlockSpec(memory_space=pltpu.VMEM)
    hbm = pl.BlockSpec(memory_space=pltpu.HBM)
    smem = pl.BlockSpec(memory_space=pltpu.SMEM)
    out = jax.ShapeDtypeStruct((rows, width), F32)
    dma = pltpu.SemaphoreType.DMA

    def blocks(n, kind=BF16):
        return pltpu.VMEM((n, 16, packed), kind)

    grads = pl.pallas_call(
        functools.partial(kernel, n_row, n_t),
        out_shape=(out, out),
        in_specs=[hbm, hbm, smem, smem],
        out_specs=(vmem, vmem),
        scratch_shapes=[
            pltpu.VMEM((rows, width), BF16),
            pltpu.VMEM((rows, width), BF16),
            pltpu.VMEM((pad, width), F32),
            pltpu.VMEM((pad, width), F32),
            pltpu.VMEM((pad, width), F32),
            pltpu.VMEM((pad, 128), F32),
            pltpu.VMEM((pad, 128), F32),
            blocks(n_i),
            blocks(n_t),
            pltpu.VMEM((n_i * pad, n_t * pad), F32),
            pltpu.VMEM((n_t * pad, n_i * pad), BF16),
            pltpu.VMEM((n_i * 16, n_t * pad), BF16),
            pltpu.VMEM((n_i * 8, n_t * pad), BF16),
            blocks(n_t),
            blocks(n_row),
            blocks(n_row, F32),
            blocks(n_row),
            pltpu.VMEM((16, packed), F32),
            blocks(n_t),
            blocks(n_row),
            blocks(n_row),
            dma((2,)), dma((4,)), dma((3 * n_row + 2 * n_t + 2,)),
            dma((n_i,)), dma((n_t,)), dma((n_t,)), dma((n_row,)), dma((1,)),
        ],
        compiler_params=pltpu.CompilerParams(
            collective_id=0, has_side_effects=True),
    )(images, texts, logarithmic_scale, similarity_bias)
    return pl.pallas_call(
        hand_over, out_shape=(out, out), in_specs=[vmem, vmem], out_specs=(vmem, vmem))(*grads)


def solution(mesh):
    return jax.shard_map(
        functools.partial(on_device, mesh.shape["row"], mesh.shape["col"]),
        mesh=mesh,
        in_specs=(P(("row", "col"), None), P(("col", "row"), None), P(), P()),
        out_specs=(P(("row", "col"), None), P(("col", "row"), None)),
        check_vma=False,
    )
```

```python
import functools

import jax
import jax.numpy as jnp
from jax import lax
from jax.experimental import pallas as pl
from jax.experimental.pallas import tpu as pltpu
from jax.sharding import PartitionSpec as P

MESH = pl.DeviceIdType.MESH
F32, BF16 = jnp.float32, jnp.bfloat16


def pack(x):
    width = x.shape[1]
    left = -(-width // 256) * 128
    right = jnp.concatenate([x[16:, left:], jnp.zeros((8, 2 * left - width), x.dtype)], axis=1)
    return x[:16], jnp.concatenate([x[16:, :left], right], axis=0)


def unpack_tail(tail, width):
    left = tail.shape[1]
    return jnp.concatenate([tail[:8], tail[8:, :width - left]], axis=1)


def unit_rows(x_ref, wide, length_ref, unit_ref, block_ref):
    rows, width = x_ref.shape
    wide[...] = jnp.zeros_like(wide)
    wide[:rows] = x_ref[...].astype(F32)
    x = wide[...]
    length = jnp.sqrt(jnp.sum(x * x, axis=1, keepdims=True) + 1e-06)
    unit = x / length
    unit_ref[...] = unit
    length_ref[...] = jnp.broadcast_to(length, length_ref.shape)
    head, tail = pack(unit)
    block_ref[:, :width] = head.astype(BF16)
    block_ref[:, width:] = tail.astype(BF16)


def all_rows(blocks, width):
    n = blocks.shape[0]
    heads = blocks[:, :, :width].reshape(n * 16, width)
    tails = [unpack_tail(blocks[k, :, width:].astype(F32), width) for k in range(n)]
    return jnp.concatenate([heads, jnp.concatenate(tails, axis=0).astype(BF16)], axis=0)


def to_blocks(partial, blocks):
    n, width = blocks.shape[0], partial.shape[1]
    for k in range(n):
        head, tail = pack(jnp.concatenate(
            [partial[16 * k:16 * k + 16], partial[16 * n + 8 * k:16 * n + 8 * k + 8]], axis=0))
        blocks[k, :, :width] = head.astype(blocks.dtype)
        blocks[k, :, width:] = tail.astype(blocks.dtype)


def member_row(index, n):
    tail = index - 16 * n
    member = jnp.where(index < 16 * n, index // 16, tail // 8)
    return member, jnp.where(index < 16 * n, index % 16, 16 + tail % 8)


def norm_back(unit, length, upstream):
    along = jnp.sum(unit * upstream, axis=1, keepdims=True)
    return (upstream - unit * along) / length


def kernel(n_row, n_t, img_ref, txt_ref, scale_ref, bias_ref, gimg_ref, gtxt_ref,
           oi, ot, xi, xt, wide, iu, tu, il, tl, gi, gt, label_ref, im, imt, wh, wl, pt, ps, po, pi, acc, rt, rs, ri,
           in_sem, out_sem, send_sem, ci, ct, ct2, ci2, pair_sem):
    rows, width = img_ref.shape
    load_t = pltpu.make_async_copy(txt_ref, xt, in_sem.at[0])
    load_i = pltpu.make_async_copy(img_ref, xi, in_sem.at[1])
    load_t.start()
    load_i.start()
    n_i = 2 * n_row
    row, col = lax.axis_index("row"), lax.axis_index("col")
    plane, core = col // 2, col % 2
    other_core = 1 - core
    me_i = core * n_row + row
    low = plane < n_t // 2
    from_end = jnp.where(low, plane, n_t - 1 - plane)
    planes = []
    for t in range(n_t - 1, 0, -1):
        t = jnp.where(t > from_end, t, t - 1)
        planes.append(jnp.where(low, t, n_t - 1 - t))

    def at_row(r):
        return (r, col)

    def at_plane(h):
        return (row, 2 * h + core)

    sibling = (row, 2 * plane + other_core)
    other_rows = [lax.rem(row + k, n_row) for k in range(1, n_row)]

    barrier = pltpu.get_barrier_semaphore()
    for place in [at_plane(h) for h in planes] + [at_row(r) for r in other_rows] + [sibling]:
        pl.semaphore_signal(barrier, inc=1, device_id=place, device_id_type=MESH)
    load_t.wait()
    unit_rows(xt, wide, tl, tu, gt.at[plane])
    load_i.wait()
    unit_rows(xi, wide, il, iu, gi.at[me_i])
    r = lax.broadcasted_iota(jnp.int32, (1, 24 * n_i), 1)
    c = lax.broadcasted_iota(jnp.int32, (24 * n_t, 1), 0)
    g, r = member_row(r, n_i)
    h, c = member_row(c, n_t)
    row_ids = ((g % n_row) * (2 * n_t) + plane * 2 + g // n_row) * rows + r
    col_ids = ((h * 2 + core) * n_row + row) * rows + c
    label = jnp.where(row_ids == col_ids, F32(1.0), F32(-1.0))
    label_ref[...] = label
    temperature = jnp.exp(jnp.full((1, 1), scale_ref[...], F32))
    pl.semaphore_wait(barrier, n_row + n_t - 1)

    sent = []

    def push(src, dst, recv, place):
        copy = pltpu.make_async_remote_copy(
            src_ref=src, dst_ref=dst, send_sem=send_sem.at[len(sent)], recv_sem=recv,
            device_id=place, device_id_type=MESH)
        copy.start()
        sent.append(copy)

    def arrived(dst, recv):
        pltpu.make_async_remote_copy(
            src_ref=dst, dst_ref=dst, send_sem=send_sem.at[0], recv_sem=recv,
            device_id=sibling, device_id_type=MESH).wait_recv()

    for h in planes:
        push(gt.at[plane], gt.at[plane], ct.at[plane], at_plane(h))
    for r in other_rows:
        push(gi.at[me_i], gi.at[me_i], ci.at[me_i], at_row(r))
    push(gi.at[me_i], gi.at[me_i], ci.at[me_i], sibling)
    for r in other_rows:
        g = core * n_row + r
        arrived(gi.at[g], ci.at[g])
        push(gi.at[g], gi.at[g], ci.at[g], sibling)
    for r in [row] + other_rows:
        g = other_core * n_row + r
        arrived(gi.at[g], ci.at[g])
    im[...] = all_rows(gi, width)
    imt[...] = im[...].T
    for h in planes[::-1]:
        arrived(gt.at[h], ct.at[h])
    texts = all_rows(gt, width)
    scores = jnp.dot(texts, imt[...], preferred_element_type=F32)
    label = label_ref[...]
    margin = label * (temperature * scores + bias_ref[...])
    weights = -label * jax.nn.sigmoid(-margin)
    to_blocks(jnp.dot(weights.astype(BF16), im[...], preferred_element_type=F32), pt)
    for h in planes:
        push(pt.at[h], rt.at[plane], ct2.at[plane], at_plane(h))

    weights = weights.T.astype(BF16)
    wh[...] = weights[:16 * n_i]
    wl[...] = weights[16 * n_i:]

    def half(c):
        head = wh[pl.ds(pl.multiple_of(c * (16 * n_row), 16), 16 * n_row)]
        tail = wl[pl.ds(pl.multiple_of(c * (8 * n_row), 16), 8 * n_row)]
        return jnp.dot(jnp.concatenate([head, tail], axis=0), texts, preferred_element_type=F32)

    to_blocks(half(other_core), ps)
    push(ps, rs, pair_sem.at[0], sibling)
    to_blocks(half(core), po)
    arrived(rs, pair_sem.at[0])
    for r in other_rows:
        pi[r] = (po[r] + rs[r].astype(F32)).astype(BF16)
        push(pi.at[r], ri.at[row], ci2.at[row], at_row(r))

    def rows_of(total):
        return temperature * jnp.concatenate([total[:, :width], unpack_tail(total[:, width:], width)], axis=0)

    acc[...] = po[row] + rs[row].astype(F32)
    for r in other_rows:
        arrived(ri.at[r], ci2.at[r])
        acc[...] += ri[r].astype(F32)
    oi[...] = norm_back(iu[...], il[:, :1], rows_of(acc[...]))[:rows]
    out_i = pltpu.make_async_copy(oi, gimg_ref, out_sem.at[0])
    out_i.start()
    acc[...] = pt[plane].astype(F32)
    for h in planes[::-1]:
        arrived(rt.at[h], ct2.at[h])
        acc[...] += rt[h].astype(F32)
    ot[...] = norm_back(tu[...], tl[:, :1], rows_of(acc[...]))[:rows]
    out_t = pltpu.make_async_copy(ot, gtxt_ref, out_sem.at[1])
    out_t.start()
    for copy in sent:
        copy.wait_send()
    out_i.wait()
    out_t.wait()


def hand_over(gimg_ref, gtxt_ref, images_ref, texts_ref):
    images_ref[...] = gimg_ref[...]
    texts_ref[...] = gtxt_ref[...]


def on_device(n_row, n_col, images, texts, logarithmic_scale, similarity_bias):
    rows, width = images.shape
    pad = 24
    packed = width + -(-width // 256) * 128
    assert 16 < rows <= pad and n_col % 2 == 0 and n_row % 2 == 0
    n_i, n_t = 2 * n_row, n_col // 2
    vmem = pl.BlockSpec(memory_space=pltpu.VMEM)
    hbm = pl.BlockSpec(memory_space=pltpu.HBM)
    smem = pl.BlockSpec(memory_space=pltpu.SMEM)
    out = jax.ShapeDtypeStruct((rows, width), F32)
    dma = pltpu.SemaphoreType.DMA

    def blocks(n, kind=BF16):
        return pltpu.VMEM((n, 16, packed), kind)

    grads = pl.pallas_call(
        functools.partial(kernel, n_row, n_t),
        out_shape=(out, out),
        in_specs=[hbm, hbm, smem, smem],
        out_specs=(hbm, hbm),
        scratch_shapes=[
            pltpu.VMEM((rows, width), F32),
            pltpu.VMEM((rows, width), F32),
            pltpu.VMEM((rows, width), BF16),
            pltpu.VMEM((rows, width), BF16),
            pltpu.VMEM((pad, width), F32),
            pltpu.VMEM((pad, width), F32),
            pltpu.VMEM((pad, width), F32),
            pltpu.VMEM((pad, 128), F32),
            pltpu.VMEM((pad, 128), F32),
            blocks(n_i),
            blocks(n_t),
            pltpu.VMEM((n_t * pad, n_i * pad), F32),
            pltpu.VMEM((n_i * pad, width), BF16),
            pltpu.VMEM((width, n_i * pad), BF16),
            pltpu.VMEM((n_i * 16, n_t * pad), BF16),
            pltpu.VMEM((n_i * 8, n_t * pad), BF16),
            blocks(n_t),
            blocks(n_row),
            blocks(n_row, F32),
            blocks(n_row),
            pltpu.VMEM((16, packed), F32),
            blocks(n_t),
            blocks(n_row),
            blocks(n_row),
            dma((2,)), dma((2,)), dma((3 * n_row + 2 * n_t + 2,)),
            dma((n_i,)), dma((n_t,)), dma((n_t,)), dma((n_row,)), dma((1,)),
        ],
        compiler_params=pltpu.CompilerParams(
            collective_id=0, has_side_effects=True),
    )(images, texts, logarithmic_scale, similarity_bias)
    return pl.pallas_call(
        hand_over, out_shape=(out, out), in_specs=[vmem, vmem], out_specs=(vmem, vmem))(*grads)


def solution(mesh):
    return jax.shard_map(
        functools.partial(on_device, mesh.shape["row"], mesh.shape["col"]),
        mesh=mesh,
        in_specs=(P(("row", "col"), None), P(("col", "row"), None), P(), P()),
        out_specs=(P(("row", "col"), None), P(("col", "row"), None)),
        check_vma=False,
    )
```

```python
import functools

import jax
import jax.numpy as jnp
from jax import lax
from jax.experimental import pallas as pl
from jax.experimental.pallas import tpu as pltpu
from jax.sharding import PartitionSpec as P

MESH = pl.DeviceIdType.MESH
F32, BF16 = jnp.float32, jnp.bfloat16


def pack(x):
    width = x.shape[1]
    left = -(-width // 256) * 128
    right = jnp.concatenate([x[16:, left:], jnp.zeros((8, 2 * left - width), x.dtype)], axis=1)
    return x[:16], jnp.concatenate([x[16:, :left], right], axis=0)


def unpack_tail(tail, width):
    left = tail.shape[1]
    return jnp.concatenate([tail[:8], tail[8:, :width - left]], axis=1)


def unit_rows(x_ref, wide, length_ref, unit_ref, block_ref):
    rows, width = x_ref.shape
    wide[...] = jnp.zeros_like(wide)
    wide[:rows] = x_ref[...].astype(F32)
    x = wide[...]
    length = jnp.sqrt(jnp.sum(x * x, axis=1, keepdims=True) + 1e-06)
    unit = x / length
    unit_ref[...] = unit
    length_ref[...] = jnp.broadcast_to(length, length_ref.shape)
    head, tail = pack(unit)
    block_ref[:, :width] = head.astype(BF16)
    block_ref[:, width:] = tail.astype(BF16)


def all_rows(blocks, width):
    n = blocks.shape[0]
    heads = blocks[:, :, :width].reshape(n * 16, width)
    tails = [unpack_tail(blocks[k, :, width:].astype(F32), width) for k in range(n)]
    return jnp.concatenate([heads, jnp.concatenate(tails, axis=0).astype(BF16)], axis=0)


def to_blocks(partial, blocks):
    n, width = blocks.shape[0], partial.shape[1]
    for k in range(n):
        head, tail = pack(jnp.concatenate(
            [partial[16 * k:16 * k + 16], partial[16 * n + 8 * k:16 * n + 8 * k + 8]], axis=0))
        blocks[k, :, :width] = head.astype(blocks.dtype)
        blocks[k, :, width:] = tail.astype(blocks.dtype)


def member_row(index, n):
    tail = index - 16 * n
    member = jnp.where(index < 16 * n, index // 16, tail // 8)
    return member, jnp.where(index < 16 * n, index % 16, 16 + tail % 8)


def norm_back(unit, length, upstream):
    along = jnp.sum(unit * upstream, axis=1, keepdims=True)
    return (upstream - unit * along) / length


def kernel(n_row, n_t, img_ref, txt_ref, scale_ref, bias_ref, gimg_ref, gtxt_ref,
           wide, iu, tu, il, tl, gi, gt, label_ref, im, imt, wh, wl, pt, ps, po, pi, acc, rt, rs, ri,
           send_sem, ci, ct, ct2, ci2, pair_sem):
    rows, width = img_ref.shape
    n_i = 2 * n_row
    row, col = lax.axis_index("row"), lax.axis_index("col")
    plane, core = col // 2, col % 2
    other_core = 1 - core
    me_i = core * n_row + row
    low = plane < n_t // 2
    from_end = jnp.where(low, plane, n_t - 1 - plane)
    planes = []
    for t in range(n_t - 1, 0, -1):
        t = jnp.where(t > from_end, t, t - 1)
        planes.append(jnp.where(low, t, n_t - 1 - t))

    def at_row(r):
        return (r, col)

    def at_plane(h):
        return (row, 2 * h + core)

    sibling = (row, 2 * plane + other_core)
    other_rows = [lax.rem(row + k, n_row) for k in range(1, n_row)]

    barrier = pltpu.get_barrier_semaphore()
    for place in [at_plane(h) for h in planes] + [at_row(r) for r in other_rows] + [sibling]:
        pl.semaphore_signal(barrier, inc=1, device_id=place, device_id_type=MESH)
    unit_rows(txt_ref, wide, tl, tu, gt.at[plane])
    unit_rows(img_ref, wide, il, iu, gi.at[me_i])
    r = lax.broadcasted_iota(jnp.int32, (1, 24 * n_i), 1)
    c = lax.broadcasted_iota(jnp.int32, (24 * n_t, 1), 0)
    g, r = member_row(r, n_i)
    h, c = member_row(c, n_t)
    row_ids = ((g % n_row) * (2 * n_t) + plane * 2 + g // n_row) * rows + r
    col_ids = ((h * 2 + core) * n_row + row) * rows + c
    label = jnp.where(row_ids == col_ids, F32(1.0), F32(-1.0))
    label_ref[...] = label
    temperature = jnp.exp(jnp.full((1, 1), scale_ref[...], F32))
    pl.semaphore_wait(barrier, n_row + n_t - 1)

    sent = []

    def push(src, dst, recv, place):
        copy = pltpu.make_async_remote_copy(
            src_ref=src, dst_ref=dst, send_sem=send_sem.at[len(sent)], recv_sem=recv,
            device_id=place, device_id_type=MESH)
        copy.start()
        sent.append(copy)

    def arrived(dst, recv):
        pltpu.make_async_remote_copy(
            src_ref=dst, dst_ref=dst, send_sem=send_sem.at[0], recv_sem=recv,
            device_id=sibling, device_id_type=MESH).wait_recv()

    for h in planes:
        push(gt.at[plane], gt.at[plane], ct.at[plane], at_plane(h))
    for r in other_rows:
        push(gi.at[me_i], gi.at[me_i], ci.at[me_i], at_row(r))
    push(gi.at[me_i], gi.at[me_i], ci.at[me_i], sibling)
    for r in other_rows:
        g = core * n_row + r
        arrived(gi.at[g], ci.at[g])
        push(gi.at[g], gi.at[g], ci.at[g], sibling)
    for r in [row] + other_rows:
        g = other_core * n_row + r
        arrived(gi.at[g], ci.at[g])
    im[...] = all_rows(gi, width)
    imt[...] = im[...].T
    for h in planes[::-1]:
        arrived(gt.at[h], ct.at[h])
    texts = all_rows(gt, width)
    scores = jnp.dot(texts, imt[...], preferred_element_type=F32)
    label = label_ref[...]
    margin = label * (temperature * scores + bias_ref[...])
    weights = -label * jax.nn.sigmoid(-margin)
    to_blocks(jnp.dot(weights.astype(BF16), im[...], preferred_element_type=F32), pt)
    for h in planes:
        push(pt.at[h], rt.at[plane], ct2.at[plane], at_plane(h))

    weights = weights.T.astype(BF16)
    wh[...] = weights[:16 * n_i]
    wl[...] = weights[16 * n_i:]

    def half(c):
        head = wh[pl.ds(pl.multiple_of(c * (16 * n_row), 16), 16 * n_row)]
        tail = wl[pl.ds(pl.multiple_of(c * (8 * n_row), 16), 8 * n_row)]
        return jnp.dot(jnp.concatenate([head, tail], axis=0), texts, preferred_element_type=F32)

    to_blocks(half(other_core), ps)
    push(ps, rs, pair_sem.at[0], sibling)
    to_blocks(half(core), po)
    arrived(rs, pair_sem.at[0])
    for r in other_rows:
        pi[r] = (po[r] + rs[r].astype(F32)).astype(BF16)
        push(pi.at[r], ri.at[row], ci2.at[row], at_row(r))

    def rows_of(total):
        return temperature * jnp.concatenate([total[:, :width], unpack_tail(total[:, width:], width)], axis=0)

    acc[...] = po[row] + rs[row].astype(F32)
    for r in other_rows:
        arrived(ri.at[r], ci2.at[r])
        acc[...] += ri[r].astype(F32)
    gimg_ref[...] = norm_back(iu[...], il[:, :1], rows_of(acc[...]))[:rows]
    acc[...] = pt[plane].astype(F32)
    for h in planes[::-1]:
        arrived(rt.at[h], ct2.at[h])
        acc[...] += rt[h].astype(F32)
    gtxt_ref[...] = norm_back(tu[...], tl[:, :1], rows_of(acc[...]))[:rows]
    for copy in sent:
        copy.wait_send()


def hand_over(gimg_ref, gtxt_ref, images_ref, texts_ref):
    images_ref[...] = gimg_ref[...]
    texts_ref[...] = gtxt_ref[...]


def on_device(n_row, n_col, images, texts, logarithmic_scale, similarity_bias):
    rows, width = images.shape
    pad = 24
    packed = width + -(-width // 256) * 128
    assert 16 < rows <= pad and n_col % 2 == 0 and n_row % 2 == 0
    n_i, n_t = 2 * n_row, n_col // 2
    vmem = pl.BlockSpec(memory_space=pltpu.VMEM)
    smem = pl.BlockSpec(memory_space=pltpu.SMEM)
    out = jax.ShapeDtypeStruct((rows, width), F32)
    dma = pltpu.SemaphoreType.DMA

    def blocks(n, kind=BF16):
        return pltpu.VMEM((n, 16, packed), kind)

    grads = pl.pallas_call(
        functools.partial(kernel, n_row, n_t),
        out_shape=(out, out),
        in_specs=[vmem, vmem, smem, smem],
        out_specs=(vmem, vmem),
        scratch_shapes=[
            pltpu.VMEM((pad, width), F32),
            pltpu.VMEM((pad, width), F32),
            pltpu.VMEM((pad, width), F32),
            pltpu.VMEM((pad, 128), F32),
            pltpu.VMEM((pad, 128), F32),
            blocks(n_i),
            blocks(n_t),
            pltpu.VMEM((n_t * pad, n_i * pad), F32),
            pltpu.VMEM((n_i * pad, width), BF16),
            pltpu.VMEM((width, n_i * pad), BF16),
            pltpu.VMEM((n_i * 16, n_t * pad), BF16),
            pltpu.VMEM((n_i * 8, n_t * pad), BF16),
            blocks(n_t),
            blocks(n_row),
            blocks(n_row, F32),
            blocks(n_row),
            pltpu.VMEM((16, packed), F32),
            blocks(n_t),
            blocks(n_row),
            blocks(n_row),
            dma((3 * n_row + 2 * n_t + 2,)),
            dma((n_i,)), dma((n_t,)), dma((n_t,)), dma((n_row,)), dma((1,)),
        ],
        compiler_params=pltpu.CompilerParams(
            collective_id=0, has_side_effects=True,
            vmem_limit_bytes=48 * 2**20),
    )(images, texts, logarithmic_scale, similarity_bias)
    return pl.pallas_call(
        hand_over, out_shape=(out, out), in_specs=[vmem, vmem], out_specs=(vmem, vmem))(*grads)


def solution(mesh):
    return jax.shard_map(
        functools.partial(on_device, mesh.shape["row"], mesh.shape["col"]),
        mesh=mesh,
        in_specs=(P(("row", "col"), None), P(("col", "row"), None), P(), P()),
        out_specs=(P(("row", "col"), None), P(("col", "row"), None)),
        check_vma=False,
    )
```

```python
import functools

import jax
import jax.numpy as jnp
from jax import lax
from jax.experimental import pallas as pl
from jax.experimental.pallas import tpu as pltpu
from jax.sharding import PartitionSpec as P

MESH = pl.DeviceIdType.MESH
F32, BF16 = jnp.float32, jnp.bfloat16


def pack(x):
    width = x.shape[1]
    left = -(-width // 256) * 128
    right = jnp.concatenate([x[16:, left:], jnp.zeros((8, 2 * left - width), x.dtype)], axis=1)
    return x[:16], jnp.concatenate([x[16:, :left], right], axis=0)


def unpack_tail(tail, width):
    left = tail.shape[1]
    return jnp.concatenate([tail[:8], tail[8:, :width - left]], axis=1)


def unit_rows(x_ref, wide, length_ref, unit_ref, block_ref):
    rows, width = x_ref.shape
    wide[...] = jnp.zeros_like(wide)
    wide[:rows] = x_ref[...].astype(F32)
    x = wide[...]
    length = jnp.sqrt(jnp.sum(x * x, axis=1, keepdims=True) + 1e-06)
    unit = x / length
    unit_ref[...] = unit
    length_ref[...] = jnp.broadcast_to(length, length_ref.shape)
    head, tail = pack(unit)
    block_ref[:, :width] = head.astype(BF16)
    block_ref[:, width:] = tail.astype(BF16)


def all_rows(blocks, width):
    n = blocks.shape[0]
    heads = blocks[:, :, :width].reshape(n * 16, width)
    tails = [unpack_tail(blocks[k, :, width:].astype(F32), width) for k in range(n)]
    return jnp.concatenate([heads, jnp.concatenate(tails, axis=0).astype(BF16)], axis=0)


def to_blocks(partial, blocks):
    n, width = blocks.shape[0], partial.shape[1]
    for k in range(n):
        head, tail = pack(jnp.concatenate(
            [partial[16 * k:16 * k + 16], partial[16 * n + 8 * k:16 * n + 8 * k + 8]], axis=0))
        blocks[k, :, :width] = head.astype(blocks.dtype)
        blocks[k, :, width:] = tail.astype(blocks.dtype)


def member_row(index, n):
    tail = index - 16 * n
    member = jnp.where(index < 16 * n, index // 16, tail // 8)
    return member, jnp.where(index < 16 * n, index % 16, 16 + tail % 8)


def norm_back(unit, length, upstream):
    along = jnp.sum(unit * upstream, axis=1, keepdims=True)
    return (upstream - unit * along) / length


def kernel(n_row, n_t, img_ref, txt_ref, scale_ref, bias_ref, gimg_ref, gtxt_ref,
           xi, xt, wide, iu, tu, il, tl, gi, gt, label_ref, wt, wh, wl, pt, ps, po, pi, acc, rt, rs, ri,
           in_sem, send_sem, ci, ct, ct2, ci2, pair_sem):
    rows, width = img_ref.shape
    load_t = pltpu.make_async_copy(txt_ref, xt, in_sem.at[0])
    load_i = pltpu.make_async_copy(img_ref, xi, in_sem.at[1])
    load_t.start()
    load_i.start()
    n_i = 2 * n_row
    row, col = lax.axis_index("row"), lax.axis_index("col")
    plane, core = col // 2, col % 2
    other_core = 1 - core
    me_i = core * n_row + row
    low = plane < n_t // 2
    from_end = jnp.where(low, plane, n_t - 1 - plane)
    planes = []
    for t in range(n_t - 1, 0, -1):
        t = jnp.where(t > from_end, t, t - 1)
        planes.append(jnp.where(low, t, n_t - 1 - t))

    def at_row(r):
        return (r, col)

    def at_plane(h):
        return (row, 2 * h + core)

    sibling = (row, 2 * plane + other_core)
    other_rows = [lax.rem(row + k, n_row) for k in range(1, n_row)]

    barrier = pltpu.get_barrier_semaphore()
    for place in [at_plane(h) for h in planes] + [at_row(r) for r in other_rows] + [sibling]:
        pl.semaphore_signal(barrier, inc=1, device_id=place, device_id_type=MESH)
    load_t.wait()
    unit_rows(xt, wide, tl, tu, gt.at[plane])
    load_i.wait()
    unit_rows(xi, wide, il, iu, gi.at[me_i])
    r = lax.broadcasted_iota(jnp.int32, (24 * n_i, 1), 0)
    c = lax.broadcasted_iota(jnp.int32, (1, 24 * n_t), 1)
    g, r = member_row(r, n_i)
    h, c = member_row(c, n_t)
    row_ids = ((g % n_row) * (2 * n_t) + plane * 2 + g // n_row) * rows + r
    col_ids = ((h * 2 + core) * n_row + row) * rows + c
    label = jnp.where(row_ids == col_ids, F32(1.0), F32(-1.0))
    label_ref[...] = label
    temperature = jnp.exp(jnp.full((1, 1), scale_ref[...], F32))
    pl.semaphore_wait(barrier, n_row + n_t - 1)

    sent = []

    def push(src, dst, recv, place):
        copy = pltpu.make_async_remote_copy(
            src_ref=src, dst_ref=dst, send_sem=send_sem.at[len(sent)], recv_sem=recv,
            device_id=place, device_id_type=MESH)
        copy.start()
        sent.append(copy)

    def arrived(dst, recv):
        pltpu.make_async_remote_copy(
            src_ref=dst, dst_ref=dst, send_sem=send_sem.at[0], recv_sem=recv,
            device_id=sibling, device_id_type=MESH).wait_recv()

    for h in planes:
        push(gt.at[plane], gt.at[plane], ct.at[plane], at_plane(h))
    for r in other_rows:
        push(gi.at[me_i], gi.at[me_i], ci.at[me_i], at_row(r))
    push(gi.at[me_i], gi.at[me_i], ci.at[me_i], sibling)
    for r in other_rows:
        g = core * n_row + r
        arrived(gi.at[g], ci.at[g])
        push(gi.at[g], gi.at[g], ci.at[g], sibling)
    for r in [row] + other_rows:
        g = other_core * n_row + r
        arrived(gi.at[g], ci.at[g])
    images = all_rows(gi, width)
    for h in planes[::-1]:
        arrived(gt.at[h], ct.at[h])
    texts = all_rows(gt, width)
    scores = lax.dot_general(images, texts, (((1,), (1,)), ((), ())), preferred_element_type=F32)
    label = label_ref[...]
    margin = label * (temperature * scores + bias_ref[...])
    weights = -label * jax.nn.sigmoid(-margin)
    wh[...] = weights[:16 * n_i].astype(BF16)
    wl[...] = weights[16 * n_i:].astype(BF16)

    def half(c):
        head = wh[pl.ds(pl.multiple_of(c * (16 * n_row), 16), 16 * n_row)]
        tail = wl[pl.ds(pl.multiple_of(c * (8 * n_row), 16), 8 * n_row)]
        return jnp.dot(jnp.concatenate([head, tail], axis=0), texts, preferred_element_type=F32)

    to_blocks(half(other_core), ps)
    push(ps, rs, pair_sem.at[0], sibling)
    wt[...] = weights.T.astype(BF16)
    to_blocks(jnp.dot(wt[...], images, preferred_element_type=F32), pt)
    for h in planes:
        push(pt.at[h], rt.at[plane], ct2.at[plane], at_plane(h))
    to_blocks(half(core), po)
    arrived(rs, pair_sem.at[0])
    for r in other_rows:
        pi[r] = (po[r] + rs[r].astype(F32)).astype(BF16)
        push(pi.at[r], ri.at[row], ci2.at[row], at_row(r))

    def rows_of(total):
        return temperature * jnp.concatenate([total[:, :width], unpack_tail(total[:, width:], width)], axis=0)

    acc[...] = po[row] + rs[row].astype(F32)
    for r in other_rows:
        arrived(ri.at[r], ci2.at[r])
        acc[...] += ri[r].astype(F32)
    gimg_ref[...] = norm_back(iu[...], il[:, :1], rows_of(acc[...]))[:rows]
    acc[...] = pt[plane].astype(F32)
    for h in planes[::-1]:
        arrived(rt.at[h], ct2.at[h])
        acc[...] += rt[h].astype(F32)
    gtxt_ref[...] = norm_back(tu[...], tl[:, :1], rows_of(acc[...]))[:rows]
    for copy in sent:
        copy.wait_send()


def hand_over(gimg_ref, gtxt_ref, images_ref, texts_ref):
    images_ref[...] = gimg_ref[...]
    texts_ref[...] = gtxt_ref[...]


def on_device(n_row, n_col, images, texts, logarithmic_scale, similarity_bias):
    rows, width = images.shape
    pad = 24
    packed = width + -(-width // 256) * 128
    assert 16 < rows <= pad and n_col % 2 == 0 and n_row % 2 == 0
    n_i, n_t = 2 * n_row, n_col // 2
    vmem = pl.BlockSpec(memory_space=pltpu.VMEM)
    hbm = pl.BlockSpec(memory_space=pltpu.HBM)
    smem = pl.BlockSpec(memory_space=pltpu.SMEM)
    out = jax.ShapeDtypeStruct((rows, width), F32)
    dma = pltpu.SemaphoreType.DMA

    def blocks(n, kind=BF16):
        return pltpu.VMEM((n, 16, packed), kind)

    grads = pl.pallas_call(
        functools.partial(kernel, n_row, n_t),
        out_shape=(out, out),
        in_specs=[hbm, hbm, smem, smem],
        out_specs=(vmem, vmem),
        scratch_shapes=[
            pltpu.VMEM((rows, width), BF16),
            pltpu.VMEM((rows, width), BF16),
            pltpu.VMEM((pad, width), F32),
            pltpu.VMEM((pad, width), F32),
            pltpu.VMEM((pad, width), F32),
            pltpu.VMEM((pad, 128), F32),
            pltpu.VMEM((pad, 128), F32),
            blocks(n_i),
            blocks(n_t),
            pltpu.VMEM((n_i * pad, n_t * pad), F32),
            pltpu.VMEM((n_t * pad, n_i * pad), BF16),
            pltpu.VMEM((n_i * 16, n_t * pad), BF16),
            pltpu.VMEM((n_i * 8, n_t * pad), BF16),
            blocks(n_t),
            blocks(n_row),
            blocks(n_row, F32),
            blocks(n_row),
            pltpu.VMEM((16, packed), F32),
            blocks(n_t),
            blocks(n_row),
            blocks(n_row),
            dma((2,)), dma((3 * n_row + 2 * n_t + 2,)),
            dma((n_i,)), dma((n_t,)), dma((n_t,)), dma((n_row,)), dma((1,)),
        ],
        compiler_params=pltpu.CompilerParams(
            collective_id=0, has_side_effects=True),
    )(images, texts, logarithmic_scale, similarity_bias)
    return pl.pallas_call(
        hand_over, out_shape=(out, out), in_specs=[vmem, vmem], out_specs=(vmem, vmem))(*grads)


def solution(mesh):
    return jax.shard_map(
        functools.partial(on_device, mesh.shape["row"], mesh.shape["col"]),
        mesh=mesh,
        in_specs=(P(("row", "col"), None), P(("col", "row"), None), P(), P()),
        out_specs=(P(("row", "col"), None), P(("col", "row"), None)),
        check_vma=False,
    )
```
